256 devices in a mesh: pair: 32 (over z, x_hi, core), panel: 8 (over x_lo, y).
Axes of the slice: x: 4 (x_hi: 2, x_lo: 2; x = x_hi * 2 + x_lo), y: 4, z: 8, core: 2. Of those that a mesh axis runs over, the one named last changes fastest.
Arguments:
- psi: bfloat16 [1536, 3072], P('pair', 'panel'), may hold values from -6 to 6
- left_ops: bfloat16 [64, 12, 2, 128, 128], P('pair'), may hold values from -0.046875 to 0.046875
- a_rows: int32 [64, 12, 2], P('pair'), may hold values from 0 to 11
- right_ops: bfloat16 [64, 3072, 3072], P('pair', 'panel'), may hold values from -0.109375 to 0.109375
- left_sizes: int32 [12], replicated, may hold values from 32 to 128
- right_sizes: int32 [24], replicated, may hold values from 32 to 128
Outputs:
- sigma: float32 [1536, 3072], P('pair', 'panel')
The draws below stay inside these ranges and needn't reach their ends.
All inputs are finite; a program needn't handle non-finite values.
Results may differ from the reference program's by a relative error of at most 0.0029.
Values may be sent and summed in bfloat16 or wider, within the bound.
No kernel may reach another device: no remote copies, remote signals or barrier semaphores. Data moves between devices by JAX's collectives and lax.ppermute only.
A program may use at most 128 MiB of HBM per device.

```python
import jax
import jax.numpy as jnp
from jax import lax

BLK = 128
KA = 2
ML = 1536
MR = 3072
PAIRS = 64
NBL = 12
NBR = 24


def with_ends(values, stream_key, smallest, top_value):
    spot = [jax.random.randint(jax.random.fold_in(stream_key, axis), (), 0, length) for axis, length in enumerate(values.shape)]
    longest = values.shape.index(max(values.shape))
    neighbour = spot[:longest] + [(spot[longest] + 1) % values.shape[longest]] + spot[longest + 1:]
    return values.at[tuple(spot)].set(smallest).at[tuple(neighbour)].set(top_value)


def levels(rng, shape, pieces, least, largest):
    level, own = 1.0, jax.random.fold_in(rng, 6)
    for position, parts in pieces:
        draws = jnp.exp(jax.random.uniform(jax.random.fold_in(own, position), (parts,), jnp.float32, least / len(pieces), largest / len(pieces)))
        level = level * jnp.repeat(draws, shape[position] // parts).reshape([-1 if axis == position else 1 for axis in range(len(shape))])
    return level


def noise(stream_key, extent, spread, reach, cuts=(), held_as=jnp.bfloat16):
    drawn = spread * jax.random.normal(stream_key, extent, jnp.float32)
    if cuts:
        drawn = drawn * levels(stream_key, extent, cuts, -0.22, 0.18)
    return jnp.clip(drawn, -reach, reach).astype(held_as)


def setup_inputs(seed: int = 0) -> dict:
    keys = jax.random.split(jax.random.key(seed), 7)
    return {
        "psi": noise(keys[0], (ML, MR), 1.0, 6.0, ((0, 32), (1, 8))),
        "left_ops": noise(keys[1], (PAIRS, NBL, KA, BLK, BLK), (BLK * KA * PAIRS) ** -0.5, 0.046875, ((0, 32),)),
        "a_rows": with_ends(jax.random.randint(keys[2], (PAIRS, NBL, KA), 0, NBL), jax.random.fold_in(keys[2], 1), 0, NBL - 1).astype(jnp.int32),
        "right_ops": noise(keys[3], (PAIRS, MR, MR), MR ** -0.5, 0.109375, ((0, 32), (1, 8))),
        "left_sizes": with_ends(jax.random.randint(keys[4], (NBL,), BLK // 4, BLK + 1), jax.random.fold_in(keys[4], 1), BLK // 4, BLK).astype(jnp.int32),
        "right_sizes": with_ends(jax.random.randint(keys[5], (NBR,), BLK // 4, BLK + 1), jax.random.fold_in(keys[5], 1), BLK // 4, BLK).astype(jnp.int32),
    }


def live_mask(sizes):
    count = sizes.shape[0]
    offsets = lax.broadcasted_iota(jnp.int32, (count, BLK), 1)
    return (offsets < sizes[:, None]).astype(jnp.float32).reshape(count * BLK)


def reference(psi, left_ops, a_rows, right_ops, left_sizes, right_sizes):
    left_live = live_mask(left_sizes)
    right_live = live_mask(right_sizes)
    masked = (psi.astype(jnp.float32) * left_live[:, None] * right_live[None, :]).astype(jnp.bfloat16)
    masked_wide = masked.astype(jnp.float32)
    block_ids = jnp.arange(NBL, dtype=jnp.int32)

    def one_pair(total, items):
        ops_left, rows, ops_right = items
        product = jnp.dot(masked_wide, ops_right.astype(jnp.float32).T, precision=lax.Precision.HIGHEST)
        product = (product * right_live[None, :]).astype(jnp.bfloat16)
        blocks = product.astype(jnp.float32).reshape(NBL, BLK, MR)
        prods = jnp.einsum("csij,cjk->csik", ops_left.astype(jnp.float32), blocks, precision=lax.Precision.HIGHEST)
        onehot = (rows[:, :, None] == block_ids[None, None, :]).astype(jnp.float32)
        placed = jnp.einsum("csb,csik->bik", onehot, prods, precision=lax.Precision.HIGHEST)
        return total + placed.reshape(ML, MR), None

    total, _ = lax.scan(one_pair, jnp.zeros((ML, MR), jnp.float32), (left_ops, a_rows, right_ops))
    return total * left_live[:, None]
```

```python
import functools

import jax
import jax.numpy as jnp
from jax import lax
from jax.experimental import pallas as pl
from jax.experimental.pallas import tpu as pltpu
from jax.sharding import PartitionSpec as P

BLK = 128
NZ, NXH, NC, NXL, NY = 8, 2, 2, 2, 4
NX = NXH * NXL
RING = 4
AXES = ("pair", "panel")
VMEM_LIMIT = 26 * 1024 * 1024
SMEM_SPEC = pl.BlockSpec(memory_space=pltpu.SMEM)
VMEM_SPEC = pl.BlockSpec(memory_space=pltpu.VMEM)
ANY_SPEC = pl.BlockSpec(memory_space=pl.ANY)


def flat(z, x, y, core):
    pair = (z * NXH + x // NXL) * NC + core
    return pair * (NXL * NY) + (x % NXL) * NY + y


def everywhere():
    return [
        (z, x, y, core) for z in range(NZ) for x in range(NX) for y in range(NY) for core in range(NC)
    ]


def core_swap(value):
    return lax.ppermute(
        value, AXES, [(flat(z, x, y, 1 - c), flat(z, x, y, c)) for z, x, y, c in everywhere()]
    )


def last_shift(value, step):
    perm = []
    for z, x, y, c in everywhere():
        source = flat(z, (x + step) % NX, y, c) if c == 0 else flat(z, x, (y + step) % NY, c)
        perm.append((source, flat(z, x, y, c)))
    return lax.ppermute(value, AXES, perm)


def exchange(copies, groups):
    return lax.all_to_all(
        copies, AXES, split_axis=0, concat_axis=0, axis_index_groups=groups, tiled=True
    )


def z_groups():
    return [
        [flat(z, x, y, c) for z in range(NZ)] for x in range(NX) for y in range(NY) for c in range(NC)
    ]


def middle_groups():
    along_y = [[flat(z, x, y, 0) for y in range(NY)] for z in range(NZ) for x in range(NX)]
    along_x = [[flat(z, x, y, 1) for x in range(NX)] for z in range(NZ) for y in range(NY)]
    return along_y + along_x


def mask_kernel(where_ref, left_ref, right_ref, psi_ref, out_ref):
    rows, cols = psi_ref.shape
    base = where_ref[0] * rows
    first = base // BLK
    second = jnp.minimum(first + 1, left_ref.shape[0] - 1)
    index = base + lax.broadcasted_iota(jnp.int32, (rows, BLK), 0)
    limit = jnp.where(
        index < (first + 1) * BLK, first * BLK + left_ref[first], (first + 1) * BLK + left_ref[second]
    )
    row_live = index < limit
    lane = lax.broadcasted_iota(jnp.int32, (rows, BLK), 1)
    for block in range(cols // BLK):
        live = row_live & (lane < right_ref[where_ref[1] * (cols // BLK) + block])
        span = slice(block * BLK, (block + 1) * BLK)
        value = psi_ref[:, span].astype(jnp.float32)
        value = jnp.where(live, value, 0.0).astype(out_ref.dtype)
        for copy in range(out_ref.shape[0]):
            out_ref[copy, :, span] = value


def mask_psi(where, left_sizes, right_sizes, psi):
    return pl.pallas_call(
        mask_kernel,
        out_shape=jax.ShapeDtypeStruct((NZ,) + psi.shape, psi.dtype),
        in_specs=[SMEM_SPEC, SMEM_SPEC, SMEM_SPEC, VMEM_SPEC],
        out_specs=VMEM_SPEC,
        name="mask_psi",
    )(where, left_sizes, right_sizes, psi)


def product_kernel(steps, first, last, where_ref, *refs):
    refs = list(refs)
    rows_ref, right_ref = (refs.pop(0), refs.pop(0)) if last else (None, None)
    acc_in = None if first else refs.pop(0)
    arrays = [refs.pop(0) for _ in steps]
    r_own, r_other = refs.pop(0), refs.pop(0)
    l_own, l_other = (refs.pop(0), refs.pop(0)) if last else (None, None)
    if last:
        keep_ref, send_ref, acc, lbuf, part, total = (refs.pop(0) for _ in range(6))
    else:
        acc = refs.pop(0)
    ubuf, rbuf, sem_u, sem_r, sem_a, sem_l = refs
    z, xh, core, xl, y = (where_ref[i] for i in range(2, 7))
    x = xh * NXL + xl
    pairs, cols, depth = r_own.shape
    group = ubuf.shape[2]

    units = []
    for array, step, start in zip(arrays, *zip(*steps)):
        for spot in range(array.shape[0]):
            middle = start + spot
            far_x, far_y = lax.rem(x + step, NX), lax.rem(y + step, NY)
            unit_x = jnp.where(core == 0, far_x, middle)
            unit_y = jnp.where(core == 0, middle, far_y)
            units.append((array, spot, unit_x, unit_y))

    def unit_copy(index):
        array, spot = units[index][:2]
        return pltpu.make_async_copy(array.at[spot], ubuf.at[index], sem_u.at[index])

    def right_copies(index):
        _, _, unit_x, unit_y = units[index]
        column = pl.multiple_of((lax.rem(unit_x, NXL) * NY + unit_y) * cols, BLK)
        slot = index % 2
        return [
            pltpu.make_async_copy(
                source.at[:, :, pl.ds(column, cols)],
                rbuf.at[slot, pl.ds(side * pairs, pairs)],
                sem_r.at[slot, side],
            )
            for side, source in enumerate((r_own, r_other))
        ]

    for copy in right_copies(0):
        copy.start()
    for index in range(len(units)):
        unit_copy(index).start()
    waits = []
    if not first:
        waits.append(pltpu.make_async_copy(acc_in, acc, sem_a))
    if last:
        waits.append(pltpu.make_async_copy(l_own, lbuf.at[pl.ds(0, pairs)], sem_l.at[0]))
        waits.append(pltpu.make_async_copy(l_other, lbuf.at[pl.ds(pairs, pairs)], sem_l.at[1]))
    for copy in waits:
        copy.start()
    if first:
        acc[...] = jnp.zeros_like(acc)
    if last:
        total[...] = jnp.zeros_like(total)
        part[...] = jnp.zeros_like(part)
    if not first:
        waits.pop(0).wait()

    for index in range(len(units)):
        if index + 1 < len(units):
            for copy in right_copies(index + 1):
                copy.start()
        unit_copy(index).wait()
        for copy in right_copies(index):
            copy.wait()
        half = units[index][2] // NXL
        left = ubuf[index].reshape(NZ * group, cols)
        for pair in range(2 * pairs):
            acc[half, pair] += lax.dot_general(
                left,
                rbuf[index % 2, pair],
                (((1,), (1,)), ((), ())),
                preferred_element_type=jnp.float32,
            )

    if not last:
        return
    blocks, ka = lbuf.shape[1:3]
    lane = lax.broadcasted_iota(jnp.int32, (1, BLK), 1)
    start = (xl * NY + y) * (cols // BLK)
    live = jnp.concatenate(
        [(lane < right_ref[start + i]).astype(jnp.float32) for i in range(cols // BLK)], axis=1
    )
    for copy in waits:
        copy.wait()

    @pl.loop(0, 2 * pairs)
    def _(pair):
        for half in range(NXH):
            for dz in range(NZ):
                rounded = (acc[half, pair, dz * group : (dz + 1) * group] * live).astype(part.dtype)
                at = ((dz * NXH + half) * NC + core) * group
                part[pl.ds(pl.multiple_of(at, 16), group), :] = rounded
        for block in range(blocks):
            result = jnp.dot(
                lbuf[pair, block].reshape(ka * BLK, BLK),
                part[block * BLK : (block + 1) * BLK],
                preferred_element_type=jnp.float32,
            )
            for s in range(ka):
                row = rows_ref[(pair * blocks + block) * ka + s]
                total[pl.ds(pl.multiple_of(row * BLK, BLK), BLK), :] += result[s * BLK : (s + 1) * BLK]

    for q in range(NZ * NXH):
        mine = pl.multiple_of((q * NC + core) * group, 16)
        theirs = pl.multiple_of((q * NC + 1 - core) * group, 16)
        keep_ref[q] = total[pl.ds(mine, group), :]
        send_ref[q] = total[pl.ds(theirs, group), :].astype(send_ref.dtype)


def product(where, acc, pieces, right, left=None, rows=None, right_sizes=None):
    arrays = [array for array, _, _ in pieces]
    steps = tuple((step, start) for _, step, start in pieces)
    first, last = acc is None, left is not None
    group, cols = arrays[0].shape[2:]
    pairs = right[0].shape[0]
    units = sum(array.shape[0] for array in arrays)
    acc_shape = (NXH, 2 * pairs, NZ * group, cols)
    operands, specs = [where], [SMEM_SPEC]
    if last:
        operands += [rows, right_sizes]
        specs += [SMEM_SPEC, SMEM_SPEC]
    rest = ([] if first else [acc]) + arrays + list(right) + (list(left) if last else [])
    operands += rest
    specs += [ANY_SPEC] * len(rest)
    scratch = []
    if last:
        blocks = left[0].shape[1]
        out_shape = (
            jax.ShapeDtypeStruct((NZ * NXH, group, cols), jnp.float32),
            jax.ShapeDtypeStruct((NZ * NXH, group, cols), jnp.bfloat16),
        )
        out_specs = (VMEM_SPEC, VMEM_SPEC)
        scratch = [
            pltpu.VMEM(acc_shape, jnp.float32),
            pltpu.VMEM((2 * pairs,) + left[0].shape[1:], jnp.bfloat16),
            pltpu.VMEM((blocks * BLK, cols), jnp.bfloat16),
            pltpu.VMEM((blocks * BLK, cols), jnp.float32),
        ]
    else:
        out_shape = jax.ShapeDtypeStruct(acc_shape, jnp.float32)
        out_specs = VMEM_SPEC
    scratch += [
        pltpu.VMEM((units, NZ, group, cols), jnp.bfloat16),
        pltpu.VMEM((2, 2 * pairs, cols, cols), jnp.bfloat16),
        pltpu.SemaphoreType.DMA((units,)),
        pltpu.SemaphoreType.DMA((2, 2)),
        pltpu.SemaphoreType.DMA,
        pltpu.SemaphoreType.DMA((2,)),
    ]
    return pl.pallas_call(
        functools.partial(product_kernel, steps, first, last),
        out_shape=out_shape,
        in_specs=specs,
        out_specs=out_specs,
        scratch_shapes=scratch,
        compiler_params=pltpu.CompilerParams(vmem_limit_bytes=VMEM_LIMIT),
        cost_estimate=pl.CostEstimate(
            flops=2 * units * 2 * pairs * NZ * group * cols * cols,
            bytes_accessed=units * 2 * pairs * cols * cols * 2 + 9_000_000,
            transcendentals=0,
        ),
        name=f"product_{units}",
    )(*operands)


def local(psi, left_ops, a_rows, right_ops, left_sizes, right_sizes):
    rows_dev = psi.shape[0]
    pair, panel = lax.axis_index("pair"), lax.axis_index("panel")
    where = jnp.stack(
        [
            pair,
            panel,
            lax.shift_right_logical(pair, 2),
            lax.shift_right_logical(pair, 1) & 1,
            pair & 1,
            lax.shift_right_logical(panel, 2),
            panel & 3,
        ]
    ).astype(jnp.int32)
    copies = mask_psi(where, left_sizes, right_sizes, psi)
    right = (right_ops, core_swap(right_ops))
    left = (left_ops, core_swap(left_ops))
    rows = jnp.concatenate([a_rows.reshape(-1), core_swap(a_rows.reshape(-1))])

    along_z = exchange(copies, z_groups())
    wide = exchange(jnp.broadcast_to(along_z[None], (RING,) + along_z.shape), middle_groups())
    plus = last_shift(wide, 1)
    minus = last_shift(wide, -1)
    acc = product(where, None, [(wide, 0, 0)], right)
    half = RING // 2
    plus, minus, acc = lax.optimization_barrier((plus, minus, acc))
    far_low = last_shift(plus[:half], 1)
    far_high = last_shift(minus[half:], -1)

    acc = product(where, acc, [(plus, 1, 0), (minus, 3, 0)], right)
    keep, send = product(
        where, acc, [(far_low, 2, 0), (far_high, 2, half)], right, left, rows, right_sizes
    )
    mine = (keep + core_swap(send).astype(jnp.float32)).astype(jnp.bfloat16)
    groups = [
        [flat(z, xh * NXL + xl, y, c) for z in range(NZ) for xh in range(NXH)]
        for c in range(NC)
        for xl in range(NXL)
        for y in range(NY)
    ]
    parts = exchange(mine, groups)
    summed = parts.astype(jnp.float32).sum(axis=0)
    index = pair * rows_dev + jnp.arange(rows_dev, dtype=jnp.int32)
    blocks = jnp.arange(left_sizes.shape[0], dtype=jnp.int32)
    limit = jnp.sum(jnp.where(index[:, None] // BLK == blocks, left_sizes + blocks * BLK, 0), axis=1)
    return jnp.where((index < limit)[:, None], summed, 0.0)


def solution(mesh):
    placed = (
        P("pair", "panel"),
        P("pair", None, None, None, None),
        P("pair", None, None),
        P("pair", "panel", None),
        P(),
        P(),
    )
    return jax.shard_map(
        local, mesh=mesh, in_specs=placed, out_specs=P("pair", "panel"), check_vma=False
    )
```

```python
import functools

import jax
import jax.numpy as jnp
from jax import lax
from jax.experimental import pallas as pl
from jax.experimental.pallas import tpu as pltpu
from jax.sharding import PartitionSpec as P

BLK = 128
NZ, NXH, NC, NXL, NY = 8, 2, 2, 2, 4
NX = NXH * NXL
RING = 4
AXES = ("pair", "panel")
VMEM_LIMIT = 32 * 1024 * 1024
SMEM_SPEC = pl.BlockSpec(memory_space=pltpu.SMEM)
VMEM_SPEC = pl.BlockSpec(memory_space=pltpu.VMEM)
ANY_SPEC = pl.BlockSpec(memory_space=pl.ANY)


def flat(z, x, y, core):
    pair = (z * NXH + x // NXL) * NC + core
    return pair * (NXL * NY) + (x % NXL) * NY + y


def everywhere():
    return [
        (z, x, y, core) for z in range(NZ) for x in range(NX) for y in range(NY) for core in range(NC)
    ]


def core_swap(value):
    return lax.ppermute(
        value, AXES, [(flat(z, x, y, 1 - c), flat(z, x, y, c)) for z, x, y, c in everywhere()]
    )


def last_shift(value, step):
    perm = []
    for z, x, y, c in everywhere():
        source = flat(z, (x + step) % NX, y, c) if c == 0 else flat(z, x, (y + step) % NY, c)
        perm.append((source, flat(z, x, y, c)))
    return lax.ppermute(value, AXES, perm)


def exchange(copies, groups):
    return lax.all_to_all(
        copies, AXES, split_axis=0, concat_axis=0, axis_index_groups=groups, tiled=True
    )


def z_groups():
    return [
        [flat(z, x, y, c) for z in range(NZ)] for x in range(NX) for y in range(NY) for c in range(NC)
    ]


def middle_groups():
    along_y = [[flat(z, x, y, 0) for y in range(NY)] for z in range(NZ) for x in range(NX)]
    along_x = [[flat(z, x, y, 1) for x in range(NX)] for z in range(NZ) for y in range(NY)]
    return along_y + along_x


def mask_kernel(where_ref, left_ref, right_ref, psi_ref, out_ref):
    rows, cols = psi_ref.shape
    base = where_ref[0] * rows
    first = base // BLK
    second = jnp.minimum(first + 1, left_ref.shape[0] - 1)
    index = base + lax.broadcasted_iota(jnp.int32, (rows, BLK), 0)
    limit = jnp.where(
        index < (first + 1) * BLK, first * BLK + left_ref[first], (first + 1) * BLK + left_ref[second]
    )
    row_live = index < limit
    lane = lax.broadcasted_iota(jnp.int32, (rows, BLK), 1)
    for block in range(cols // BLK):
        live = row_live & (lane < right_ref[where_ref[1] * (cols // BLK) + block])
        span = slice(block * BLK, (block + 1) * BLK)
        value = psi_ref[:, span].astype(jnp.float32)
        value = jnp.where(live, value, 0.0).astype(out_ref.dtype)
        for copy in range(out_ref.shape[0]):
            out_ref[copy, :, span] = value


def mask_psi(where, left_sizes, right_sizes, psi):
    return pl.pallas_call(
        mask_kernel,
        out_shape=jax.ShapeDtypeStruct((NZ,) + psi.shape, psi.dtype),
        in_specs=[SMEM_SPEC, SMEM_SPEC, SMEM_SPEC, VMEM_SPEC],
        out_specs=VMEM_SPEC,
        name="mask_psi",
    )(where, left_sizes, right_sizes, psi)


def product_kernel(steps, first, last, where_ref, *refs):
    refs = list(refs)
    rows_ref, right_ref = (refs.pop(0), refs.pop(0)) if last else (None, None)
    acc_in = None if first else refs.pop(0)
    arrays = [refs.pop(0) for _ in steps]
    right = (refs.pop(0), refs.pop(0))
    left = (refs.pop(0), refs.pop(0)) if last else None
    acc = refs.pop(0)
    xh, core, xl, y = (where_ref[i] for i in range(3, 7))
    x = xh * NXL + xl
    pairs, cols, _ = right[0].shape
    group = arrays[0].shape[2]

    acc[...] = jnp.zeros_like(acc) if first else acc_in[...]
    for array, (step, start) in zip(arrays, steps):
        far_x, far_y = lax.rem(x + step, NX), lax.rem(y + step, NY)

        @pl.loop(0, array.shape[0] // 2)
        def _(two):
            columns = []
            for spot in range(2):
                middle = start + 2 * two + spot
                unit_x = jnp.where(core == 0, far_x, middle)
                unit_y = jnp.where(core == 0, middle, far_y)
                columns.append(pl.multiple_of((lax.rem(unit_x, NXL) * NY + unit_y) * cols, BLK))
            half = unit_x // NXL
            wide = jnp.concatenate(
                [array[2 * two + spot].reshape(NZ * group, cols) for spot in range(2)], axis=1
            )
            for side in range(2):
                operator = jnp.concatenate(
                    [right[side][:, :, pl.ds(c, cols)].reshape(pairs * cols, cols) for c in columns], axis=1
                )
                acc[half, side] += lax.dot_general(
                    wide, operator, (((1,), (1,)), ((), ())), preferred_element_type=jnp.float32
                )

    if not last:
        return
    keep_ref, send_ref, part, total = refs
    _, blocks, ka = left[0].shape[:3]
    lane = lax.broadcasted_iota(jnp.int32, (1, BLK), 1)
    start = (xl * NY + y) * (cols // BLK)
    live = jnp.concatenate(
        [(lane < right_ref[start + i]).astype(jnp.float32) for i in range(cols // BLK)], axis=1
    )
    total[...] = jnp.zeros_like(total)
    part[...] = jnp.zeros_like(part)
    for side in range(2):

        @pl.loop(0, pairs)
        def _(pair):
            column = pl.multiple_of(pair * cols, BLK)
            for half in range(NXH):
                for dz in range(NZ):
                    term = acc[half, side, pl.ds(dz * group, group), pl.ds(column, cols)]
                    at = ((dz * NXH + half) * NC + core) * group
                    part[pair, pl.ds(pl.multiple_of(at, 16), group), :] = (term * live).astype(part.dtype)
            for block in range(blocks):
                result = jnp.dot(
                    left[side][pair, block].reshape(ka * BLK, BLK),
                    part[pair, block * BLK : (block + 1) * BLK],
                    preferred_element_type=jnp.float32,
                )
                for s in range(ka):
                    row = rows_ref[((side * pairs + pair) * blocks + block) * ka + s]
                    at = pl.multiple_of(row * BLK, BLK)
                    total[pl.ds(at, BLK), :] += result[s * BLK : (s + 1) * BLK]

    for q in range(NZ * NXH):
        mine = pl.multiple_of((q * NC + core) * group, 16)
        theirs = pl.multiple_of((q * NC + 1 - core) * group, 16)
        keep_ref[q] = total[pl.ds(mine, group), :]
        send_ref[q] = total[pl.ds(theirs, group), :].astype(send_ref.dtype)


def product(where, acc, pieces, right, left=None, rows=None, right_sizes=None):
    arrays = [array for array, _, _ in pieces]
    steps = tuple((step, start) for _, step, start in pieces)
    first, last = acc is None, left is not None
    group, cols = arrays[0].shape[2:]
    pairs = right[0].shape[0]
    units = sum(array.shape[0] for array in arrays)
    acc_shape = (NXH, 2, NZ * group, pairs * cols)
    operands, specs = [where], [SMEM_SPEC]
    if last:
        operands += [rows, right_sizes]
        specs += [SMEM_SPEC, SMEM_SPEC]
    aliases = {} if first else {len(operands): 0}
    rest = ([] if first else [acc]) + arrays + list(right) + (list(left) if last else [])
    operands += rest
    specs += [VMEM_SPEC] * len(rest)
    scratch = []
    out_shape = [jax.ShapeDtypeStruct(acc_shape, jnp.float32)]
    if last:
        blocks = left[0].shape[1]
        out_shape += [
            jax.ShapeDtypeStruct((NZ * NXH, group, cols), jnp.float32),
            jax.ShapeDtypeStruct((NZ * NXH, group, cols), jnp.bfloat16),
        ]
        scratch = [
            pltpu.VMEM((pairs, blocks * BLK, cols), jnp.bfloat16),
            pltpu.VMEM((blocks * BLK, cols), jnp.float32),
        ]
    return pl.pallas_call(
        functools.partial(product_kernel, steps, first, last),
        out_shape=out_shape,
        in_specs=specs,
        out_specs=[VMEM_SPEC] * len(out_shape),
        scratch_shapes=scratch,
        input_output_aliases=aliases,
        compiler_params=pltpu.CompilerParams(vmem_limit_bytes=VMEM_LIMIT),
        cost_estimate=pl.CostEstimate(
            flops=2 * units * 2 * pairs * NZ * group * cols * cols,
            bytes_accessed=units * 2 * pairs * cols * cols * 2,
            transcendentals=0,
        ),
        name=f"product_{units}",
    )(*operands)


def local(psi, left_ops, a_rows, right_ops, left_sizes, right_sizes):
    rows_dev = psi.shape[0]
    pair, panel = lax.axis_index("pair"), lax.axis_index("panel")
    where = jnp.stack(
        [
            pair,
            panel,
            lax.shift_right_logical(pair, 2),
            lax.shift_right_logical(pair, 1) & 1,
            pair & 1,
            lax.shift_right_logical(panel, 2),
            panel & 3,
        ]
    ).astype(jnp.int32)
    copies = mask_psi(where, left_sizes, right_sizes, psi)
    right = (right_ops, core_swap(right_ops))
    left = (left_ops, core_swap(left_ops))
    rows = jnp.concatenate([a_rows.reshape(-1), core_swap(a_rows.reshape(-1))])

    along_z = exchange(copies, z_groups())
    wide = exchange(jnp.broadcast_to(along_z[None], (RING,) + along_z.shape), middle_groups())
    plus = last_shift(wide, 1)
    minus = last_shift(wide, -1)
    (acc,) = product(where, None, [(wide, 0, 0)], right)
    half = RING // 2
    plus, minus, acc, rows = lax.optimization_barrier((plus, minus, acc, rows))
    far_low = last_shift(plus[:half], 1)
    far_high = last_shift(minus[half:], -1)

    (acc,) = product(where, acc, [(plus, 1, 0), (minus, 3, 0)], right)
    _, keep, send = product(
        where, acc, [(far_low, 2, 0), (far_high, 2, half)], right, left, rows, right_sizes
    )
    mine = (keep + core_swap(send).astype(jnp.float32)).astype(jnp.bfloat16)
    groups = [
        [flat(z, xh * NXL + xl, y, c) for z in range(NZ) for xh in range(NXH)]
        for c in range(NC)
        for xl in range(NXL)
        for y in range(NY)
    ]
    parts = exchange(mine, groups)
    summed = parts.astype(jnp.float32).sum(axis=0)
    index = pair * rows_dev + jnp.arange(rows_dev, dtype=jnp.int32)
    blocks = jnp.arange(left_sizes.shape[0], dtype=jnp.int32)
    limit = jnp.sum(jnp.where(index[:, None] // BLK == blocks, left_sizes + blocks * BLK, 0), axis=1)
    return jnp.where((index < limit)[:, None], summed, 0.0)


def solution(mesh):
    placed = (
        P("pair", "panel"),
        P("pair", None, None, None, None),
        P("pair", None, None),
        P("pair", "panel", None),
        P(),
        P(),
    )
    return jax.shard_map(
        local, mesh=mesh, in_specs=placed, out_specs=P("pair", "panel"), check_vma=False
    )
```

```python
import functools

import jax
import jax.numpy as jnp
from jax import lax
from jax.experimental import pallas as pl
from jax.experimental.pallas import tpu as pltpu
from jax.sharding import PartitionSpec as P

BLK = 128
NZ, NXH, NC, NXL, NY = 8, 2, 2, 2, 4
NX = NXH * NXL
RING = 4
AXES = ("pair", "panel")
VMEM_LIMIT = 32 * 1024 * 1024
SMEM_SPEC = pl.BlockSpec(memory_space=pltpu.SMEM)
VMEM_SPEC = pl.BlockSpec(memory_space=pltpu.VMEM)
ANY_SPEC = pl.BlockSpec(memory_space=pl.ANY)


def flat(z, x, y, core):
    pair = (z * NXH + x // NXL) * NC + core
    return pair * (NXL * NY) + (x % NXL) * NY + y


def everywhere():
    return [
        (z, x, y, core) for z in range(NZ) for x in range(NX) for y in range(NY) for core in range(NC)
    ]


def core_swap(value):
    return lax.ppermute(
        value, AXES, [(flat(z, x, y, 1 - c), flat(z, x, y, c)) for z, x, y, c in everywhere()]
    )


def last_shift(value, step):
    perm = []
    for z, x, y, c in everywhere():
        source = flat(z, (x + step) % NX, y, c) if c == 0 else flat(z, x, (y + step) % NY, c)
        perm.append((source, flat(z, x, y, c)))
    return lax.ppermute(value, AXES, perm)


def exchange(copies, groups):
    return lax.all_to_all(
        copies, AXES, split_axis=0, concat_axis=0, axis_index_groups=groups, tiled=True
    )


def z_groups():
    return [
        [flat(z, x, y, c) for z in range(NZ)] for x in range(NX) for y in range(NY) for c in range(NC)
    ]


def middle_groups():
    along_y = [[flat(z, x, y, 0) for y in range(NY)] for z in range(NZ) for x in range(NX)]
    along_x = [[flat(z, x, y, 1) for x in range(NX)] for z in range(NZ) for y in range(NY)]
    return along_y + along_x


def position():
    pair, panel = lax.axis_index("pair"), lax.axis_index("panel")
    return pair // (NXH * NC), (pair // NC) % NXH, pair % NC, panel // NY, panel % NY


def mask_kernel(left_ref, right_ref, psi_ref, out_ref):
    rows, cols = psi_ref.shape
    base = lax.axis_index("pair") * rows
    panel = lax.axis_index("panel")
    first = base // BLK
    second = jnp.minimum(first + 1, left_ref.shape[0] - 1)
    index = base + lax.broadcasted_iota(jnp.int32, (rows, BLK), 0)
    limit = jnp.where(
        index < (first + 1) * BLK, first * BLK + left_ref[first], (first + 1) * BLK + left_ref[second]
    )
    row_live = index < limit
    lane = lax.broadcasted_iota(jnp.int32, (rows, BLK), 1)
    for block in range(cols // BLK):
        live = row_live & (lane < right_ref[panel * (cols // BLK) + block])
        span = slice(block * BLK, (block + 1) * BLK)
        value = psi_ref[:, span].astype(jnp.float32)
        value = jnp.where(live, value, 0.0).astype(out_ref.dtype)
        for copy in range(out_ref.shape[0]):
            out_ref[copy, :, span] = value


def mask_psi(left_sizes, right_sizes, psi):
    return pl.pallas_call(
        mask_kernel,
        out_shape=jax.ShapeDtypeStruct((NZ,) + psi.shape, psi.dtype),
        in_specs=[SMEM_SPEC, SMEM_SPEC, VMEM_SPEC],
        out_specs=VMEM_SPEC,
        name="mask_psi",
    )(left_sizes, right_sizes, psi)


def product_kernel(steps, first, last, *refs):
    refs = list(refs)
    rows_ref, right_ref = (refs.pop(0), refs.pop(0)) if last else (None, None)
    acc_in = None if first else refs.pop(0)
    arrays = [refs.pop(0) for _ in steps]
    right = (refs.pop(0), refs.pop(0))
    left = (refs.pop(0), refs.pop(0)) if last else None
    _, xh, core, xl, y = position()
    x = xh * NXL + xl
    pairs, cols, _ = right[0].shape
    group = arrays[0].shape[2]
    if last:
        keep_ref, send_ref, rbuf, sem_r, lbuf, sem_l, part, total = refs
    else:
        acc, rbuf, sem_r = refs

    twos = []
    copies = []
    for array, (step, start) in zip(arrays, steps):
        far_x, far_y = lax.rem(x + step, NX), lax.rem(y + step, NY)
        for spot in range(0, array.shape[0], 2):
            for side in range(2):
                copies.append([])
                for way in range(2):
                    middle = start + spot + way
                    unit_x = jnp.where(core == 0, far_x, middle)
                    unit_y = jnp.where(core == 0, middle, far_y)
                    column = pl.multiple_of((lax.rem(unit_x, NXL) * NY + unit_y) * cols, BLK)
                    copies[-1].append(
                        pltpu.make_async_copy(
                            right[side].at[:, :, pl.ds(column, cols)],
                            rbuf.at[len(twos), side, :, :, pl.ds(way * cols, cols)],
                            sem_r.at[len(twos), side, way],
                        )
                    )
            twos.append((array, spot, unit_x // NXL))
    for copy in sum(copies, []):
        copy.start()

    def wide(array, spot):
        return jnp.concatenate(
            [array[spot + way].reshape(NZ * group, cols) for way in range(2)], axis=1
        )

    def times(left_side, right_side):
        return lax.dot_general(
            left_side, right_side, (((1,), (1,)), ((), ())), preferred_element_type=jnp.float32
        )

    def operator(index, side):
        return rbuf[index, side].reshape(pairs * cols, 2 * cols)

    if not last:
        acc[...] = jnp.zeros_like(acc) if first else acc_in[...]
        for index, (array, spot, half) in enumerate(twos):
            for side in range(2):
                for copy in copies[2 * index + side]:
                    copy.wait()

            @pl.loop(0, 2)
            def _(side):
                acc[half, side] += times(wide(array, spot), operator(index, side))

        return

    left_copies = [
        pltpu.make_async_copy(left[side], lbuf.at[pl.ds(side * pairs, pairs)], sem_l.at[side])
        for side in range(2)
    ]
    for copy in left_copies:
        copy.start()
    blocks, ka = lbuf.shape[1:3]
    lane = lax.broadcasted_iota(jnp.int32, (1, BLK), 1)
    start = (xl * NY + y) * (cols // BLK)
    live = jnp.concatenate(
        [(lane < right_ref[start + i]).astype(jnp.float32) for i in range(cols // BLK)], axis=1
    )
    total[...] = jnp.zeros_like(total)
    part[...] = jnp.zeros_like(part)
    for copy in sum(copies, []):
        copy.wait()

    def place(half, side, sums):
        for pair in range(pairs):
            rounded = (sums[:, pair * cols : (pair + 1) * cols] * live).astype(part.dtype)
            for dz in range(NZ):
                at = ((dz * NXH + half) * NC + core) * group
                part[side * pairs + pair, pl.ds(pl.multiple_of(at, 16), group), :] = rounded[
                    dz * group : (dz + 1) * group
                ]

    @pl.loop(0, 2)
    def _(side):
        @pl.when(core == 0)
        def _():
            far = 1 - xh
            place(xh, side, acc_in[xh, side])
            left_side = jnp.concatenate([wide(array, spot) for array, spot, _ in twos], axis=1)
            right_side = jnp.concatenate([operator(index, side) for index in range(len(twos))], axis=1)
            place(far, side, acc_in[far, side] + times(left_side, right_side))

        @pl.when(core == 1)
        def _():
            for index, (array, spot, half) in enumerate(twos):
                place(half, side, acc_in[half, side] + times(wide(array, spot), operator(index, side)))

    for copy in left_copies:
        copy.wait()

    @pl.loop(0, 2 * pairs)
    def _(pair):
        for block in range(blocks):
            result = jnp.dot(
                lbuf[pair, block].reshape(ka * BLK, BLK),
                part[pair, block * BLK : (block + 1) * BLK],
                preferred_element_type=jnp.float32,
            )
            for s in range(ka):
                row = rows_ref[(pair * blocks + block) * ka + s]
                total[pl.ds(pl.multiple_of(row * BLK, BLK), BLK), :] += result[s * BLK : (s + 1) * BLK]

    for q in range(NZ * NXH):
        mine = pl.multiple_of((q * NC + core) * group, 16)
        theirs = pl.multiple_of((q * NC + 1 - core) * group, 16)
        keep_ref[q] = total[pl.ds(mine, group), :]
        send_ref[q] = total[pl.ds(theirs, group), :].astype(send_ref.dtype)


def product(acc, pieces, right, left=None, rows=None, right_sizes=None):
    arrays = [array for array, _, _ in pieces]
    steps = tuple((step, start) for _, step, start in pieces)
    first, last = acc is None, left is not None
    group, cols = arrays[0].shape[2:]
    pairs = right[0].shape[0]
    units = sum(array.shape[0] for array in arrays)
    acc_shape = (NXH, 2, NZ * group, pairs * cols)
    operands = [rows, right_sizes] if last else []
    specs = [SMEM_SPEC] * len(operands)
    aliases = {} if first or last else {len(operands): 0}
    near = ([] if first else [acc]) + arrays
    away = list(right) + (list(left) if last else [])
    operands += near + away
    specs += [VMEM_SPEC] * len(near) + [ANY_SPEC] * len(away)
    scratch = [
        pltpu.VMEM((units // 2, 2, pairs, cols, 2 * cols), jnp.bfloat16),
        pltpu.SemaphoreType.DMA((units // 2, 2, 2)),
    ]
    if last:
        blocks = left[0].shape[1]
        out_shape = [
            jax.ShapeDtypeStruct((NZ * NXH, group, cols), jnp.float32),
            jax.ShapeDtypeStruct((NZ * NXH, group, cols), jnp.bfloat16),
        ]
        scratch += [
            pltpu.VMEM((2 * pairs,) + left[0].shape[1:], jnp.bfloat16),
            pltpu.SemaphoreType.DMA((2,)),
            pltpu.VMEM((2 * pairs, blocks * BLK, cols), jnp.bfloat16),
            pltpu.VMEM((blocks * BLK, cols), jnp.float32),
        ]
    else:
        out_shape = [jax.ShapeDtypeStruct(acc_shape, jnp.float32)]
    return pl.pallas_call(
        functools.partial(product_kernel, steps, first, last),
        out_shape=out_shape,
        in_specs=specs,
        out_specs=[VMEM_SPEC] * len(out_shape),
        scratch_shapes=scratch,
        input_output_aliases=aliases,
        compiler_params=pltpu.CompilerParams(vmem_limit_bytes=VMEM_LIMIT),
        cost_estimate=pl.CostEstimate(
            flops=2 * units * 2 * pairs * NZ * group * cols * cols,
            bytes_accessed=units * 2 * pairs * cols * cols * 2,
            transcendentals=0,
        ),
        name=f"product_{units}",
    )(*operands)


def local(psi, left_ops, a_rows, right_ops, left_sizes, right_sizes):
    rows_dev = psi.shape[0]
    pair = lax.axis_index("pair")
    copies = mask_psi(left_sizes, right_sizes, psi)
    right = (right_ops, core_swap(right_ops))
    left = (left_ops, core_swap(left_ops))
    rows = jnp.concatenate([a_rows.reshape(-1), core_swap(a_rows.reshape(-1))])

    along_z = exchange(copies, z_groups())
    wide = exchange(jnp.broadcast_to(along_z[None], (RING,) + along_z.shape), middle_groups())
    plus = last_shift(wide, 1)
    minus = last_shift(wide, -1)
    (acc,) = product(None, [(wide, 0, 0)], right)
    half = RING // 2
    plus, minus, acc, rows = lax.optimization_barrier((plus, minus, acc, rows))
    far_low = last_shift(plus[:half], 1)
    far_high = last_shift(minus[half:], -1)

    (acc,) = product(acc, [(plus, 1, 0), (minus, 3, 0)], right)
    keep, send = product(
        acc, [(far_low, 2, 0), (far_high, 2, half)], right, left, rows, right_sizes
    )
    mine = (keep + core_swap(send).astype(jnp.float32)).astype(jnp.bfloat16)
    groups = [
        [flat(z, xh * NXL + xl, y, c) for z in range(NZ) for xh in range(NXH)]
        for c in range(NC)
        for xl in range(NXL)
        for y in range(NY)
    ]
    parts = exchange(mine, groups)
    summed = parts.astype(jnp.float32).sum(axis=0)
    index = pair * rows_dev + jnp.arange(rows_dev, dtype=jnp.int32)
    blocks = jnp.arange(left_sizes.shape[0], dtype=jnp.int32)
    limit = jnp.sum(jnp.where(index[:, None] // BLK == blocks, left_sizes + blocks * BLK, 0), axis=1)
    return jnp.where((index < limit)[:, None], summed, 0.0)


def solution(mesh):
    placed = (
        P("pair", "panel"),
        P("pair", None, None, None, None),
        P("pair", None, None),
        P("pair", "panel", None),
        P(),
        P(),
    )
    return jax.shard_map(
        local, mesh=mesh, in_specs=placed, out_specs=P("pair", "panel"), check_vma=False
    )
```

```python
import functools

import jax
import jax.numpy as jnp
from jax import lax
from jax.experimental import pallas as pl
from jax.experimental.pallas import tpu as pltpu
from jax.sharding import PartitionSpec as P

BLK = 128
NZ, NXH, NC, NXL, NY = 8, 2, 2, 2, 4
NX = NXH * NXL
RING = 4
AXES = ("pair", "panel")
VMEM_LIMIT = 32 * 1024 * 1024
SMEM_SPEC = pl.BlockSpec(memory_space=pltpu.SMEM)
VMEM_SPEC = pl.BlockSpec(memory_space=pltpu.VMEM)
HBM_SPEC = pl.BlockSpec(memory_space=pltpu.HBM)


def flat(z, x, y, core):
    pair = (z * NXH + x // NXL) * NC + core
    return pair * (NXL * NY) + (x % NXL) * NY + y


def everywhere():
    return [
        (z, x, y, core) for z in range(NZ) for x in range(NX) for y in range(NY) for core in range(NC)
    ]


def core_swap(value):
    return lax.ppermute(
        value, AXES, [(flat(z, x, y, 1 - c), flat(z, x, y, c)) for z, x, y, c in everywhere()]
    )


def last_shift(value, step):
    perm = []
    for z, x, y, c in everywhere():
        source = flat(z, (x + step) % NX, y, c) if c == 0 else flat(z, x, (y + step) % NY, c)
        perm.append((source, flat(z, x, y, c)))
    return lax.ppermute(value, AXES, perm)


def exchange(copies, groups):
    return lax.all_to_all(
        copies, AXES, split_axis=0, concat_axis=0, axis_index_groups=groups, tiled=True
    )


def z_groups():
    return [
        [flat(z, x, y, c) for z in range(NZ)] for x in range(NX) for y in range(NY) for c in range(NC)
    ]


def middle_groups():
    along_y = [[flat(z, x, y, 0) for y in range(NY)] for z in range(NZ) for x in range(NX)]
    along_x = [[flat(z, x, y, 1) for x in range(NX)] for z in range(NZ) for y in range(NY)]
    return along_y + along_x


def position():
    pair, panel = lax.axis_index("pair"), lax.axis_index("panel")
    return pair // (NXH * NC), (pair // NC) % NXH, pair % NC, panel // NY, panel % NY


def mask_kernel(left_ref, right_ref, psi_ref, out_ref):
    rows, cols = psi_ref.shape
    base = lax.axis_index("pair") * rows
    panel = lax.axis_index("panel")
    first = base // BLK
    second = jnp.minimum(first + 1, left_ref.shape[0] - 1)
    index = base + lax.broadcasted_iota(jnp.int32, (rows, BLK), 0)
    limit = jnp.where(
        index < (first + 1) * BLK, first * BLK + left_ref[first], (first + 1) * BLK + left_ref[second]
    )
    row_live = index < limit
    lane = lax.broadcasted_iota(jnp.int32, (rows, BLK), 1)
    for block in range(cols // BLK):
        live = row_live & (lane < right_ref[panel * (cols // BLK) + block])
        span = slice(block * BLK, (block + 1) * BLK)
        value = psi_ref[:, span].astype(jnp.float32)
        value = jnp.where(live, value, 0.0).astype(out_ref.dtype)
        for copy in range(out_ref.shape[0]):
            out_ref[copy, :, span] = value


def mask_psi(left_sizes, right_sizes, psi):
    return pl.pallas_call(
        mask_kernel,
        out_shape=jax.ShapeDtypeStruct((NZ,) + psi.shape, psi.dtype),
        in_specs=[SMEM_SPEC, SMEM_SPEC, VMEM_SPEC],
        out_specs=VMEM_SPEC,
        name="mask_psi",
    )(left_sizes, right_sizes, psi)


def plan_kernel(own_ref, other_ref, slots_ref, rows_ref, next_ref):
    shape = own_ref.shape
    count = own_ref.size
    slots = [
        (side, pair, block, s)
        for side in range(2)
        for pair in range(shape[0])
        for block in range(shape[1])
        for s in range(shape[2])
    ]

    def row_of(slot):
        return (own_ref, other_ref)[slot[0]][slot[1], slot[2], slot[3]]

    for place in range(slots_ref.shape[0]):
        slots_ref[place] = 2 * count
    for place in range(rows_ref.shape[0]):
        rows_ref[place] = 0
    for row in range(shape[1]):
        next_ref[row] = 0
    for slot in slots:
        row = row_of(slot)
        next_ref[row] = next_ref[row] + 1
    start = jnp.int32(0)
    for row in range(shape[1]):
        pairs = (next_ref[row] + 1) // 2
        next_ref[row] = 2 * start

        @pl.loop(0, pairs)
        def _(i):
            rows_ref[start + i] = row

        start = start + pairs
    for number, slot in enumerate(slots):
        row = row_of(slot)
        place = next_ref[row]
        slots_ref[place] = number
        next_ref[row] = place + 1


def plan(own, other):
    pairs = own.size + own.shape[1] // 2
    return pl.pallas_call(
        plan_kernel,
        out_shape=(
            jax.ShapeDtypeStruct((2 * pairs,), jnp.int32),
            jax.ShapeDtypeStruct((pairs,), jnp.int32),
        ),
        in_specs=[SMEM_SPEC, SMEM_SPEC],
        out_specs=(SMEM_SPEC, SMEM_SPEC),
        scratch_shapes=[pltpu.SMEM((own.shape[1],), jnp.int32)],
        name="plan",
    )(own, other)


def two_specs(steps, counts):
    return [
        (number, spot, step, start + spot)
        for number, ((step, start), count) in enumerate(zip(steps, counts))
        for spot in range(0, count, 2)
    ]


def two_copies(twos, right, buffer, sem):
    _, xh, core, xl, y = position()
    x = xh * NXL + xl
    cols = right[0].shape[1]
    copies, halves = [], []
    for index, (_, _, step, place) in enumerate(twos):
        far_x, far_y = lax.rem(x + step, NX), lax.rem(y + step, NY)
        copies.append([])
        for way in range(2):
            unit_x = jnp.where(core == 0, far_x, place + way)
            unit_y = jnp.where(core == 0, place + way, far_y)
            column = pl.multiple_of((lax.rem(unit_x, NXL) * NY + unit_y) * cols, BLK)
            for side in range(2):
                copies[-1].append(
                    pltpu.make_async_copy(
                        right[side].at[:, :, pl.ds(column, cols)],
                        buffer.at[index, side, :, :, pl.ds(way * cols, cols)],
                        sem.at[index, side, way],
                    )
                )
        halves.append(unit_x // NXL)
    return copies, halves


def wide(array, spot):
    rows = array.shape[1] * array.shape[2]
    return jnp.concatenate([array[spot + way].reshape(rows, array.shape[3]) for way in range(2)], axis=1)


def times(left_side, right_side):
    return lax.dot_general(
        left_side, right_side, (((1,), (1,)), ((), ())), preferred_element_type=jnp.float32
    )


def operator(buffer, index, side):
    return buffer[index, side].reshape(buffer.shape[2] * buffer.shape[3], buffer.shape[4])


def sums_kernel(steps, ahead, *refs):
    refs = list(refs)
    acc_in = refs.pop(0) if ahead else None
    arrays = [refs.pop(0) for _ in steps]
    right = (refs.pop(0), refs.pop(0))
    left = (refs.pop(0), refs.pop(0)) if ahead else None
    acc = refs.pop(0)
    if ahead:
        far_ref, left_ref = refs.pop(0), refs.pop(0)
        far_sem, left_sem = refs.pop(), refs.pop()
    rbuf, sem = refs
    twos = two_specs(steps, [array.shape[0] for array in arrays])
    copies, halves = two_copies(twos, right, rbuf, sem)
    later = []
    if ahead:
        later = sum(two_copies(two_specs(ahead, [RING // 2] * 2), right, far_ref, far_sem)[0], [])
        count = left[0].shape[0]
        for side in range(2):
            later.append(
                pltpu.make_async_copy(
                    left[side], left_ref.at[pl.ds(side * count, count)], left_sem.at[side]
                )
            )
        left_ref[2 * count] = jnp.zeros(left_ref.shape[1:], left_ref.dtype)
    for copy in sum(copies, []) + later:
        copy.start()
    acc[...] = acc_in[...] if ahead else jnp.zeros_like(acc)
    for index, (number, spot, _, _) in enumerate(twos):
        for copy in copies[index]:
            copy.wait()

        @pl.loop(0, 2)
        def _(side):
            acc[halves[index], side] += times(wide(arrays[number], spot), operator(rbuf, index, side))

    for copy in later:
        copy.wait()


def sums(acc, pieces, right, left=None, ahead=()):
    arrays = [array for array, _, _ in pieces]
    steps = tuple((step, start) for _, step, start in pieces)
    group, cols = arrays[0].shape[2:]
    pairs = right[0].shape[0]
    units = sum(array.shape[0] for array in arrays)
    out_shape = [jax.ShapeDtypeStruct((NXH, 2, NZ * group, pairs * cols), jnp.float32)]
    scratch = [
        pltpu.VMEM((units // 2, 2, pairs, cols, 2 * cols), jnp.bfloat16),
        pltpu.SemaphoreType.DMA((units // 2, 2, 2)),
    ]
    near, away = arrays, list(right)
    if ahead:
        near, away = [acc] + arrays, list(right) + list(left)
        out_shape += [
            jax.ShapeDtypeStruct((2, 2, pairs, cols, 2 * cols), jnp.bfloat16),
            jax.ShapeDtypeStruct((2 * left[0].shape[0] + 1,) + left[0].shape[1:], jnp.bfloat16),
        ]
        scratch += [pltpu.SemaphoreType.DMA((2,)), pltpu.SemaphoreType.DMA((2, 2, 2))]
    return pl.pallas_call(
        functools.partial(sums_kernel, steps, ahead),
        out_shape=out_shape,
        in_specs=[VMEM_SPEC] * len(near) + [HBM_SPEC] * len(away),
        out_specs=[VMEM_SPEC] * len(out_shape),
        scratch_shapes=scratch,
        input_output_aliases={0: 0} if ahead else {},
        compiler_params=pltpu.CompilerParams(vmem_limit_bytes=VMEM_LIMIT),
        cost_estimate=pl.CostEstimate(
            flops=2 * units * 2 * pairs * NZ * group * cols * cols,
            bytes_accessed=units * 2 * pairs * cols * cols * 2,
            transcendentals=0,
        ),
        name=f"sums_{units}",
    )(*near, *away)


UNROLL = 6


def terms_kernel(steps, slots_ref, rows_ref, right_ref, acc, low, high, far_ref, left_ref, *refs):
    keep_ref, send_ref, part, total = refs
    _, xh, core, xl, y = position()
    arrays = (low, high)
    group, cols = low.shape[2:]
    pairs = far_ref.shape[2]
    twos = two_specs(steps, [array.shape[0] for array in arrays])
    lane = lax.broadcasted_iota(jnp.int32, (1, BLK), 1)
    start = (xl * NY + y) * (cols // BLK)
    live = jnp.concatenate(
        [(lane < right_ref[start + i]).astype(jnp.float32) for i in range(cols // BLK)], axis=1
    )
    height = total.shape[0]
    total[...] = jnp.zeros_like(total)
    for pair in range(2 * pairs):
        for q in range(NZ * NXH):
            at = pl.multiple_of(pair * height + (q * NC + 1 - core) * group, 16)
            part[pl.ds(at, group), :] = jnp.zeros((group, cols), part.dtype)

    def place(half, side, values):
        for pair in range(pairs):
            rounded = (values[:, pair * cols : (pair + 1) * cols] * live).astype(part.dtype)
            for dz in range(NZ):
                at = (side * pairs + pair) * height + ((dz * NXH + half) * NC + core) * group
                part[pl.ds(pl.multiple_of(at, 16), group), :] = rounded[dz * group : (dz + 1) * group]

    @pl.loop(0, 2)
    def _(side):
        @pl.when(core == 0)
        def _():
            far = 1 - xh
            place(xh, side, acc[xh, side])
            left_side = jnp.concatenate([wide(arrays[n], spot) for n, spot, _, _ in twos], axis=1)
            right_side = jnp.concatenate([operator(far_ref, i, side) for i in range(len(twos))], axis=1)
            place(far, side, acc[far, side] + times(left_side, right_side))

        @pl.when(core == 1)
        def _():
            for index, (n, spot, _, middle) in enumerate(twos):
                half = middle // NXL
                place(half, side, acc[half, side] + times(wide(arrays[n], spot), operator(far_ref, index, side)))

    last_block = 2 * pairs * height // BLK - 1

    @pl.loop(0, rows_ref.shape[0] // UNROLL)
    def _(step):
        for turn in range(UNROLL):
            number = step * UNROLL + turn
            slots = [slots_ref[2 * number + way] for way in range(2)]
            blocks = [jnp.minimum(slot // 2, last_block) for slot in slots]
            result = jnp.dot(
                jnp.concatenate([left_ref[slot] for slot in slots], axis=1),
                jnp.concatenate(
                    [part[pl.ds(pl.multiple_of(block * BLK, BLK), BLK), :] for block in blocks], axis=0
                ),
                preferred_element_type=jnp.float32,
            )
            total[pl.ds(pl.multiple_of(rows_ref[number] * BLK, BLK), BLK), :] += result

    for q in range(NZ * NXH):
        mine = pl.multiple_of((q * NC + core) * group, 16)
        theirs = pl.multiple_of((q * NC + 1 - core) * group, 16)
        keep_ref[q] = total[pl.ds(mine, group), :]
        send_ref[q] = total[pl.ds(theirs, group), :].astype(send_ref.dtype)


def terms(steps, slots, rows, right_sizes, acc, low, high, far, left):
    group, cols = low.shape[2:]
    height = NZ * NXH * NC * group
    pairs = 2 * far.shape[2]
    assert rows.shape[0] % UNROLL == 0
    return pl.pallas_call(
        functools.partial(terms_kernel, steps),
        out_shape=(
            jax.ShapeDtypeStruct((NZ * NXH, group, cols), jnp.float32),
            jax.ShapeDtypeStruct((NZ * NXH, group, cols), jnp.bfloat16),
        ),
        in_specs=[SMEM_SPEC] * 3 + [VMEM_SPEC] * 5,
        out_specs=(VMEM_SPEC, VMEM_SPEC),
        scratch_shapes=[
            pltpu.VMEM((pairs * height, cols), jnp.bfloat16),
            pltpu.VMEM((height, cols), jnp.float32),
        ],
        compiler_params=pltpu.CompilerParams(vmem_limit_bytes=VMEM_LIMIT),
        name="terms",
    )(slots, rows, right_sizes, acc, low, high, far, left)


def local(psi, left_ops, a_rows, right_ops, left_sizes, right_sizes):
    rows_dev = psi.shape[0]
    pair = lax.axis_index("pair")
    copies = mask_psi(left_sizes, right_sizes, psi)
    right = (right_ops, core_swap(right_ops))
    flat_left = left_ops.reshape((-1, BLK, BLK))
    left = (flat_left, core_swap(flat_left))
    slots, rows = plan(a_rows, core_swap(a_rows))

    along_z = exchange(copies, z_groups())
    near = exchange(jnp.broadcast_to(along_z[None], (RING,) + along_z.shape), middle_groups())
    plus = last_shift(near, 1)
    minus = last_shift(near, -1)
    (acc,) = sums(None, [(near, 0, 0)], right)
    half = RING // 2
    plus, minus, acc, slots, rows = lax.optimization_barrier((plus, minus, acc, slots, rows))
    far_low = last_shift(plus[:half], 1)
    far_high = last_shift(minus[half:], -1)
    last_steps = ((2, 0), (2, half))
    acc, far, both = sums(acc, [(plus, 1, 0), (minus, 3, 0)], right, left, last_steps)
    keep, send = terms(last_steps, slots, rows, right_sizes, acc, far_low, far_high, far, both)
    mine = (keep + core_swap(send).astype(jnp.float32)).astype(jnp.bfloat16)
    groups = [
        [flat(z, xh * NXL + xl, y, c) for z in range(NZ) for xh in range(NXH)]
        for c in range(NC)
        for xl in range(NXL)
        for y in range(NY)
    ]
    parts = exchange(mine, groups)
    summed = parts.astype(jnp.float32).sum(axis=0)
    index = pair * rows_dev + jnp.arange(rows_dev, dtype=jnp.int32)
    blocks = jnp.arange(left_sizes.shape[0], dtype=jnp.int32)
    limit = jnp.sum(jnp.where(index[:, None] // BLK == blocks, left_sizes + blocks * BLK, 0), axis=1)
    return jnp.where((index < limit)[:, None], summed, 0.0)


def solution(mesh):
    placed = (
        P("pair", "panel"),
        P("pair", None, None, None, None),
        P("pair", None, None),
        P("pair", "panel", None),
        P(),
        P(),
    )
    return jax.shard_map(
        local, mesh=mesh, in_specs=placed, out_specs=P("pair", "panel"), check_vma=False
    )
```

```python
import functools

import jax
import jax.numpy as jnp
from jax import lax
from jax.experimental import pallas as pl
from jax.experimental.pallas import tpu as pltpu
from jax.sharding import PartitionSpec as P

BLK = 128
NZ, NXH, NC, NXL, NY = 8, 2, 2, 2, 4
NX = NXH * NXL
RING = 4
AXES = ("pair", "panel")
VMEM_LIMIT = 28 * 1024 * 1024
SMALL_LIMIT = 2 * 1024 * 1024
SMEM_SPEC = pl.BlockSpec(memory_space=pltpu.SMEM)
VMEM_SPEC = pl.BlockSpec(memory_space=pltpu.VMEM)
HBM_SPEC = pl.BlockSpec(memory_space=pltpu.HBM)


def flat(z, x, y, core):
    pair = (z * NXH + x // NXL) * NC + core
    return pair * (NXL * NY) + (x % NXL) * NY + y


def everywhere():
    return [
        (z, x, y, core) for z in range(NZ) for x in range(NX) for y in range(NY) for core in range(NC)
    ]


def core_swap(value):
    return lax.ppermute(
        value, AXES, [(flat(z, x, y, 1 - c), flat(z, x, y, c)) for z, x, y, c in everywhere()]
    )


def last_shift(value, step):
    perm = []
    for z, x, y, c in everywhere():
        source = flat(z, (x + step) % NX, y, c) if c == 0 else flat(z, x, (y + step) % NY, c)
        perm.append((source, flat(z, x, y, c)))
    return lax.ppermute(value, AXES, perm)


def exchange(copies, groups):
    return lax.all_to_all(
        copies, AXES, split_axis=0, concat_axis=0, axis_index_groups=groups, tiled=True
    )


def z_groups():
    return [
        [flat(z, x, y, c) for z in range(NZ)] for x in range(NX) for y in range(NY) for c in range(NC)
    ]


def middle_groups():
    along_y = [[flat(z, x, y, 0) for y in range(NY)] for z in range(NZ) for x in range(NX)]
    along_x = [[flat(z, x, y, 1) for x in range(NX)] for z in range(NZ) for y in range(NY)]
    return along_y + along_x


def position():
    pair, panel = lax.axis_index("pair"), lax.axis_index("panel")
    return pair // (NXH * NC), (pair // NC) % NXH, pair % NC, panel // NY, panel % NY


def row_live(base, left_ref, count):
    first = base // BLK
    second = jnp.minimum(first + 1, left_ref.shape[0] - 1)
    index = base + lax.broadcasted_iota(jnp.int32, (count, 1), 0)
    end = (first + 1) * BLK
    return index < jnp.where(index < end, first * BLK + left_ref[first], end + left_ref[second])


def mask_kernel(left_ref, right_ref, psi_ref, out_ref):
    rows, cols = psi_ref.shape
    panel = lax.axis_index("panel")
    rows_live = row_live(lax.axis_index("pair") * rows, left_ref, rows)
    lane = lax.broadcasted_iota(jnp.int32, (rows, BLK), 1)
    for block in range(cols // BLK):
        live = rows_live & (lane < right_ref[panel * (cols // BLK) + block])
        span = slice(block * BLK, (block + 1) * BLK)
        value = psi_ref[:, span].astype(jnp.float32)
        value = jnp.where(live, value, 0.0).astype(out_ref.dtype)
        for copy in range(out_ref.shape[0]):
            out_ref[copy, :, span] = value


def mask_psi(left_sizes, right_sizes, psi):
    return pl.pallas_call(
        mask_kernel,
        out_shape=jax.ShapeDtypeStruct((NZ,) + psi.shape, psi.dtype),
        in_specs=[SMEM_SPEC, SMEM_SPEC, VMEM_SPEC],
        out_specs=VMEM_SPEC,
        compiler_params=pltpu.CompilerParams(vmem_limit_bytes=SMALL_LIMIT),
        name="mask_psi",
    )(left_sizes, right_sizes, psi)


def plan_kernel(own_ref, other_ref, slots_ref, rows_ref, next_ref):
    shape = own_ref.shape
    count = own_ref.size
    slots = [
        (side, pair, block, s)
        for side in range(2)
        for pair in range(shape[0])
        for block in range(shape[1])
        for s in range(shape[2])
    ]

    def row_of(slot):
        return (own_ref, other_ref)[slot[0]][slot[1], slot[2], slot[3]]

    for place in range(slots_ref.shape[0]):
        slots_ref[place] = 2 * count
    for place in range(rows_ref.shape[0]):
        rows_ref[place] = 0
    for row in range(shape[1]):
        next_ref[row] = 0
    for slot in slots:
        row = row_of(slot)
        next_ref[row] = next_ref[row] + 1
    start = jnp.int32(0)
    for row in range(shape[1]):
        pairs = (next_ref[row] + 1) // 2
        next_ref[row] = 2 * start

        @pl.loop(0, pairs)
        def _(i):
            rows_ref[start + i] = row

        start = start + pairs
    for number, slot in enumerate(slots):
        row = row_of(slot)
        place = next_ref[row]
        slots_ref[place] = number
        next_ref[row] = place + 1


def plan(own, other):
    pairs = own.size + own.shape[1] // 2
    return pl.pallas_call(
        plan_kernel,
        out_shape=(
            jax.ShapeDtypeStruct((2 * pairs,), jnp.int32),
            jax.ShapeDtypeStruct((pairs,), jnp.int32),
        ),
        in_specs=[SMEM_SPEC, SMEM_SPEC],
        out_specs=(SMEM_SPEC, SMEM_SPEC),
        scratch_shapes=[pltpu.SMEM((own.shape[1],), jnp.int32)],
        compiler_params=pltpu.CompilerParams(vmem_limit_bytes=SMALL_LIMIT),
        name="plan",
    )(own, other)


def two_specs(steps, counts):
    return [
        (number, spot, step, start + spot)
        for number, ((step, start), count) in enumerate(zip(steps, counts))
        for spot in range(0, count, 2)
    ]


def two_copies(twos, right, buffer, sem):
    _, xh, core, xl, y = position()
    x = xh * NXL + xl
    cols = right[0].shape[1]
    copies, halves = [], []
    for index, (_, _, step, place) in enumerate(twos):
        far_x, far_y = lax.rem(x + step, NX), lax.rem(y + step, NY)
        copies.append([])
        for way in range(2):
            unit_x = jnp.where(core == 0, far_x, place + way)
            unit_y = jnp.where(core == 0, place + way, far_y)
            column = pl.multiple_of((lax.rem(unit_x, NXL) * NY + unit_y) * cols, BLK)
            for side in range(2):
                copies[-1].append(
                    pltpu.make_async_copy(
                        right[side].at[:, :, pl.ds(column, cols)],
                        buffer.at[index, side, :, :, pl.ds(way * cols, cols)],
                        sem.at[index, side, way],
                    )
                )
        halves.append(unit_x // NXL)
    return copies, halves


def wide(array, spot):
    rows = array.shape[1] * array.shape[2]
    return jnp.concatenate([array[spot + way].reshape(rows, array.shape[3]) for way in range(2)], axis=1)


def times(left_side, right_side):
    return lax.dot_general(
        left_side, right_side, (((1,), (1,)), ((), ())), preferred_element_type=jnp.float32
    )


def operator(buffer, index, side):
    return buffer[index, side].reshape(buffer.shape[2] * buffer.shape[3], buffer.shape[4])


def sums_kernel(steps, ahead, *refs):
    refs = list(refs)
    acc_in = refs.pop(0) if ahead else None
    arrays = [refs.pop(0) for _ in steps]
    right = (refs.pop(0), refs.pop(0))
    left = None if ahead else (refs.pop(0), refs.pop(0))
    acc, later_ref, rbuf, sem, later_sem = refs
    twos = two_specs(steps, [array.shape[0] for array in arrays])
    copies, halves = two_copies(twos, right, rbuf, sem)
    if ahead:
        later = sum(two_copies(two_specs(ahead, [RING // 2] * 2), right, later_ref, later_sem)[0], [])
    else:
        count = left[0].shape[0]
        later = [
            pltpu.make_async_copy(
                left[side], later_ref.at[pl.ds(side * count, count)], later_sem.at[side]
            )
            for side in range(2)
        ]
        later_ref[2 * count] = jnp.zeros(later_ref.shape[1:], later_ref.dtype)
    for copy in sum(copies, []) + later:
        copy.start()
    acc[...] = acc_in[...] if ahead else jnp.zeros_like(acc)
    for index, (number, spot, _, _) in enumerate(twos):
        for copy in copies[index]:
            copy.wait()

        @pl.loop(0, 2)
        def _(side):
            acc[halves[index], side] += times(wide(arrays[number], spot), operator(rbuf, index, side))

    for copy in later:
        copy.wait()


def sums(acc, pieces, right, left=None, ahead=()):
    arrays = [array for array, _, _ in pieces]
    steps = tuple((step, start) for _, step, start in pieces)
    group, cols = arrays[0].shape[2:]
    pairs = right[0].shape[0]
    units = sum(array.shape[0] for array in arrays)
    near, away = ([acc] if ahead else []) + arrays, list(right) + ([] if ahead else list(left))
    if ahead:
        later = (2, 2, pairs, cols, 2 * cols)
    else:
        later = (2 * left[0].shape[0] + 1,) + left[0].shape[1:]
    return pl.pallas_call(
        functools.partial(sums_kernel, steps, ahead),
        out_shape=[
            jax.ShapeDtypeStruct((NXH, 2, NZ * group, pairs * cols), jnp.float32),
            jax.ShapeDtypeStruct(later, jnp.bfloat16),
        ],
        in_specs=[VMEM_SPEC] * len(near) + [HBM_SPEC] * len(away),
        out_specs=[VMEM_SPEC] * 2,
        scratch_shapes=[
            pltpu.VMEM((units // 2, 2, pairs, cols, 2 * cols), jnp.bfloat16),
            pltpu.SemaphoreType.DMA((units // 2, 2, 2)),
            pltpu.SemaphoreType.DMA((2, 2, 2) if ahead else (2,)),
        ],
        input_output_aliases={0: 0} if ahead else {},
        compiler_params=pltpu.CompilerParams(vmem_limit_bytes=VMEM_LIMIT),
        cost_estimate=pl.CostEstimate(
            flops=2 * units * 2 * pairs * NZ * group * cols * cols,
            bytes_accessed=units * 2 * pairs * cols * cols * 2,
            transcendentals=0,
        ),
        name=f"sums_{units}",
    )(*near, *away)


UNROLL = 6


def terms_kernel(steps, slots_ref, rows_ref, sizes_ref, right_ref, acc, low, high, far_ref, left_ref, *refs):
    keep_ref, send_ref, part, total = refs
    _, xh, core, xl, y = position()
    arrays = (low, high)
    group, cols = low.shape[2:]
    pairs = far_ref.shape[2]
    twos = two_specs(steps, [array.shape[0] for array in arrays])
    lane = lax.broadcasted_iota(jnp.int32, (1, BLK), 1)
    start = (xl * NY + y) * (cols // BLK)
    live = jnp.concatenate(
        [(lane < right_ref[start + i]).astype(jnp.float32) for i in range(cols // BLK)], axis=1
    )
    height = total.shape[0]
    total[...] = jnp.zeros_like(total)
    for pair in range(2 * pairs):
        for q in range(NZ * NXH):
            at = pl.multiple_of(pair * height + (q * NC + 1 - core) * group, 16)
            part[pl.ds(at, group), :] = jnp.zeros((group, cols), part.dtype)

    def place(half, side, values):
        for pair in range(pairs):
            rounded = (values[:, pair * cols : (pair + 1) * cols] * live).astype(part.dtype)
            for dz in range(NZ):
                at = (side * pairs + pair) * height + ((dz * NXH + half) * NC + core) * group
                part[pl.ds(pl.multiple_of(at, 16), group), :] = rounded[dz * group : (dz + 1) * group]

    @pl.loop(0, 2)
    def _(side):
        @pl.when(core == 0)
        def _():
            far = 1 - xh
            place(xh, side, acc[xh, side])
            left_side = jnp.concatenate([wide(arrays[n], spot) for n, spot, _, _ in twos], axis=1)
            right_side = jnp.concatenate([operator(far_ref, i, side) for i in range(len(twos))], axis=1)
            place(far, side, acc[far, side] + times(left_side, right_side))

        @pl.when(core == 1)
        def _():
            for index, (n, spot, _, middle) in enumerate(twos):
                half = middle // NXL
                place(half, side, acc[half, side] + times(wide(arrays[n], spot), operator(far_ref, index, side)))

    last_block = 2 * pairs * height // BLK - 1

    @pl.loop(0, rows_ref.shape[0] // UNROLL)
    def _(step):
        for turn in range(UNROLL):
            number = step * UNROLL + turn
            slots = [slots_ref[2 * number + way] for way in range(2)]
            blocks = [jnp.minimum(slot // 2, last_block) for slot in slots]
            result = jnp.dot(
                jnp.concatenate([left_ref[slot] for slot in slots], axis=1),
                jnp.concatenate(
                    [part[pl.ds(pl.multiple_of(block * BLK, BLK), BLK), :] for block in blocks], axis=0
                ),
                preferred_element_type=jnp.float32,
            )
            total[pl.ds(pl.multiple_of(rows_ref[number] * BLK, BLK), BLK), :] += result

    for q in range(NZ * NXH):
        mine = pl.multiple_of((q * NC + core) * group, 16)
        theirs = pl.multiple_of((q * NC + 1 - core) * group, 16)
        keep_ref[q] = jnp.where(row_live(mine, sizes_ref, group), total[pl.ds(mine, group), :], 0.0)
        other = jnp.where(row_live(theirs, sizes_ref, group), total[pl.ds(theirs, group), :], 0.0)
        send_ref[q] = other.astype(send_ref.dtype)


def terms(steps, slots, rows, left_sizes, right_sizes, acc, low, high, far, left):
    group, cols = low.shape[2:]
    height = NZ * NXH * NC * group
    pairs = 2 * far.shape[2]
    assert rows.shape[0] % UNROLL == 0
    return pl.pallas_call(
        functools.partial(terms_kernel, steps),
        out_shape=(
            jax.ShapeDtypeStruct((NZ * NXH, group, cols), jnp.float32),
            jax.ShapeDtypeStruct((NZ * NXH, group, cols), jnp.bfloat16),
        ),
        in_specs=[SMEM_SPEC] * 4 + [VMEM_SPEC] * 5,
        out_specs=(VMEM_SPEC, VMEM_SPEC),
        scratch_shapes=[
            pltpu.VMEM((pairs * height, cols), jnp.bfloat16),
            pltpu.VMEM((height, cols), jnp.float32),
        ],
        compiler_params=pltpu.CompilerParams(vmem_limit_bytes=VMEM_LIMIT),
        name="terms",
    )(slots, rows, left_sizes, right_sizes, acc, low, high, far, left)


def local(psi, left_ops, a_rows, right_ops, left_sizes, right_sizes):
    copies = mask_psi(left_sizes, right_sizes, psi)
    right = (right_ops, core_swap(right_ops))
    flat_left = left_ops.reshape((-1, BLK, BLK))
    left = (flat_left, core_swap(flat_left))
    slots, rows = plan(a_rows, core_swap(a_rows))

    along_z = exchange(copies, z_groups())
    near = exchange(jnp.broadcast_to(along_z[None], (RING,) + along_z.shape), middle_groups())
    plus = last_shift(near, 1)
    minus = last_shift(near, -1)
    acc, both = sums(None, [(near, 0, 0)], right, left)
    half = RING // 2
    plus, minus, acc, slots, rows = lax.optimization_barrier((plus, minus, acc, slots, rows))
    far_low = last_shift(plus[:half], 1)
    far_high = last_shift(minus[half:], -1)
    last_steps = ((2, 0), (2, half))
    acc, far = sums(acc, [(plus, 1, 0), (minus, 3, 0)], right, ahead=last_steps)
    keep, send = terms(
        last_steps, slots, rows, left_sizes, right_sizes, acc, far_low, far_high, far, both
    )
    mine = (keep + core_swap(send).astype(jnp.float32)).astype(jnp.bfloat16)
    groups = [
        [flat(z, xh * NXL + xl, y, c) for z in range(NZ) for xh in range(NXH)]
        for c in range(NC)
        for xl in range(NXL)
        for y in range(NY)
    ]
    parts = exchange(mine, groups)
    return parts.astype(jnp.float32).sum(axis=0)


def solution(mesh):
    placed = (
        P("pair", "panel"),
        P("pair", None, None, None, None),
        P("pair", None, None),
        P("pair", "panel", None),
        P(),
        P(),
    )
    return jax.shard_map(
        local, mesh=mesh, in_specs=placed, out_specs=P("pair", "panel"), check_vma=False
    )
```

```python
import functools

import jax
import jax.numpy as jnp
from jax import lax
from jax.experimental import pallas as pl
from jax.experimental.pallas import tpu as pltpu
from jax.sharding import PartitionSpec as P

BLK = 128
NZ, NXH, NC, NXL, NY = 8, 2, 2, 2, 4
NX = NXH * NXL
AXES = ("pair", "panel")
VMEM_LIMIT = 28 * 1024 * 1024
SMALL_LIMIT = 2 * 1024 * 1024
SMEM_SPEC = pl.BlockSpec(memory_space=pltpu.SMEM)
VMEM_SPEC = pl.BlockSpec(memory_space=pltpu.VMEM)
HBM_SPEC = pl.BlockSpec(memory_space=pltpu.HBM)


def flat(z, x, y, core):
    pair = (z * NXH + x // NXL) * NC + core
    return pair * (NXL * NY) + (x % NXL) * NY + y


def everywhere():
    return [
        (z, x, y, core) for z in range(NZ) for x in range(NX) for y in range(NY) for core in range(NC)
    ]


def core_swap(value):
    return lax.ppermute(
        value, AXES, [(flat(z, x, y, 1 - c), flat(z, x, y, c)) for z, x, y, c in everywhere()]
    )


def partner(value, ring, step):
    perm = []
    for z, x, y, c in everywhere():
        along_x = (ring == "last") == (c == 0)
        source = flat(z, x ^ step, y, c) if along_x else flat(z, x, y ^ step, c)
        perm.append((source, flat(z, x, y, c)))
    return lax.ppermute(value, AXES, perm)


def exchange(copies, groups):
    return lax.all_to_all(
        copies, AXES, split_axis=0, concat_axis=0, axis_index_groups=groups, tiled=True
    )


def z_groups():
    return [
        [flat(z, x, y, c) for z in range(NZ)] for x in range(NX) for y in range(NY) for c in range(NC)
    ]


def position():
    pair, panel = lax.axis_index("pair"), lax.axis_index("panel")
    return pair // (NXH * NC), (pair // NC) % NXH, pair % NC, panel // NY, panel % NY


def row_live(base, left_ref, count):
    first = base // BLK
    second = jnp.minimum(first + 1, left_ref.shape[0] - 1)
    index = base + lax.broadcasted_iota(jnp.int32, (count, 1), 0)
    end = (first + 1) * BLK
    return index < jnp.where(index < end, first * BLK + left_ref[first], end + left_ref[second])


def mask_kernel(left_ref, right_ref, psi_ref, out_ref):
    rows, cols = psi_ref.shape
    panel = lax.axis_index("panel")
    rows_live = row_live(lax.axis_index("pair") * rows, left_ref, rows)
    lane = lax.broadcasted_iota(jnp.int32, (rows, BLK), 1)
    for block in range(cols // BLK):
        live = rows_live & (lane < right_ref[panel * (cols // BLK) + block])
        span = slice(block * BLK, (block + 1) * BLK)
        value = psi_ref[:, span].astype(jnp.float32)
        value = jnp.where(live, value, 0.0).astype(out_ref.dtype)
        for copy in range(out_ref.shape[0]):
            out_ref[copy, :, span] = value


def mask_psi(left_sizes, right_sizes, psi):
    return pl.pallas_call(
        mask_kernel,
        out_shape=jax.ShapeDtypeStruct((NZ,) + psi.shape, psi.dtype),
        in_specs=[SMEM_SPEC, SMEM_SPEC, VMEM_SPEC],
        out_specs=VMEM_SPEC,
        name="mask_psi",
    )(left_sizes, right_sizes, psi)


def plan_kernel(own_ref, other_ref, slots_ref, rows_ref, next_ref):
    shape = own_ref.shape
    count = own_ref.size
    slots = [
        (side, pair, block, s)
        for side in range(2)
        for pair in range(shape[0])
        for block in range(shape[2])
        for s in range(shape[1])
    ]

    def row_of(slot):
        return (own_ref, other_ref)[slot[0]][slot[1], slot[3], slot[2]]

    for place in range(slots_ref.shape[0]):
        slots_ref[place] = 2 * count
    for place in range(rows_ref.shape[0]):
        rows_ref[place] = 0
    for row in range(shape[2]):
        next_ref[row] = 0
    for slot in slots:
        row = row_of(slot)
        next_ref[row] = next_ref[row] + 1
    start = jnp.int32(0)
    for row in range(shape[2]):
        pairs = (next_ref[row] + 1) // 2
        next_ref[row] = 2 * start

        @pl.loop(0, pairs)
        def _(i):
            rows_ref[start + i] = row

        start = start + pairs
    for number, slot in enumerate(slots):
        row = row_of(slot)
        place = next_ref[row]
        slots_ref[place] = number
        next_ref[row] = place + 1


def plan(own, other):
    pairs = own.size + own.shape[2] // 2
    return pl.pallas_call(
        plan_kernel,
        out_shape=(
            jax.ShapeDtypeStruct((2 * pairs,), jnp.int32),
            jax.ShapeDtypeStruct((pairs,), jnp.int32),
        ),
        in_specs=[SMEM_SPEC, SMEM_SPEC],
        out_specs=(SMEM_SPEC, SMEM_SPEC),
        scratch_shapes=[pltpu.SMEM((own.shape[2],), jnp.int32)],
        compiler_params=pltpu.CompilerParams(vmem_limit_bytes=SMALL_LIMIT),
        name="plan",
    )(own, other)


NEAR, AWAY = (0, 1), (3, 2)


def two_copies(twos, right, buffer, sem):
    _, xh, core, xl, y = position()
    x = xh * NXL + xl
    cols = right[0].shape[1]
    copies, halves = [], []
    for index, (step, places) in enumerate(twos):
        copies.append([])
        for way, place in enumerate(places):
            unit_x = jnp.where(core == 0, x ^ step, x ^ place)
            unit_y = jnp.where(core == 0, y ^ place, y ^ step)
            column = pl.multiple_of((lax.rem(unit_x, NXL) * NY + unit_y) * cols, BLK)
            for side in range(2):
                copies[-1].append(
                    pltpu.make_async_copy(
                        right[side].at[:, :, pl.ds(column, cols)],
                        buffer.at[index, side, :, :, pl.ds(way * cols, cols)],
                        sem.at[index, side, way],
                    )
                )
        halves.append(unit_x // NXL)
    return copies, halves


def wide(array):
    rows = array.shape[1] * array.shape[2]
    return jnp.concatenate([array[way].reshape(rows, array.shape[3]) for way in range(2)], axis=1)


def times(left_side, right_side):
    return lax.dot_general(
        left_side, right_side, (((1,), (1,)), ((), ())), preferred_element_type=jnp.float32
    )


def operator(buffer, index, side):
    return buffer[index, side].reshape(buffer.shape[2] * buffer.shape[3], buffer.shape[4])


def sums_kernel(twos, ahead, *refs):
    refs = list(refs)
    acc_in = refs.pop(0) if ahead else None
    arrays = [refs.pop(0) for _ in twos]
    right = (refs.pop(0), refs.pop(0))
    left = None if ahead else (refs.pop(0), refs.pop(0))
    acc, later_ref, rbuf, sem, later_sem = refs
    copies, halves = two_copies(twos, right, rbuf, sem)
    if ahead:
        later = sum(two_copies(ahead, right, later_ref, later_sem)[0], [])
    else:
        count = left[0].shape[0]
        later = [
            pltpu.make_async_copy(
                left[side], later_ref.at[pl.ds(side * count, count)], later_sem.at[side]
            )
            for side in range(2)
        ]
        later_ref[2 * count] = jnp.zeros(later_ref.shape[1:], later_ref.dtype)
    for copy in sum(copies, []) + later:
        copy.start()
    acc[...] = acc_in[...] if ahead else jnp.zeros_like(acc)
    for index, array in enumerate(arrays):
        for copy in copies[index]:
            copy.wait()

        @pl.loop(0, 2)
        def _(side):
            acc[halves[index], side] += times(wide(array), operator(rbuf, index, side))

    for copy in later:
        copy.wait()


def sums(acc, pieces, right, left=None, ahead=()):
    arrays = [array for array, _, _ in pieces]
    twos = tuple((step, places) for _, step, places in pieces)
    group, cols = arrays[0].shape[2:]
    pairs = right[0].shape[0]
    units = 2 * len(arrays)
    near, away = ([acc] if ahead else []) + arrays, list(right) + ([] if ahead else list(left))
    if ahead:
        later = (2, 2, pairs, cols, 2 * cols)
    else:
        later = (2 * left[0].shape[0] + 1,) + left[0].shape[1:]
    return pl.pallas_call(
        functools.partial(sums_kernel, twos, ahead),
        out_shape=[
            jax.ShapeDtypeStruct((NXH, 2, NZ * group, pairs * cols), jnp.float32),
            jax.ShapeDtypeStruct(later, jnp.bfloat16),
        ],
        in_specs=[VMEM_SPEC] * len(near) + [HBM_SPEC] * len(away),
        out_specs=[VMEM_SPEC] * 2,
        scratch_shapes=[
            pltpu.VMEM((units // 2, 2, pairs, cols, 2 * cols), jnp.bfloat16),
            pltpu.SemaphoreType.DMA((units // 2, 2, 2)),
            pltpu.SemaphoreType.DMA((2, 2, 2) if ahead else (2,)),
        ],
        input_output_aliases={0: 0} if ahead else {},
        compiler_params=pltpu.CompilerParams(vmem_limit_bytes=VMEM_LIMIT),
        cost_estimate=pl.CostEstimate(
            flops=2 * units * 2 * pairs * NZ * group * cols * cols,
            bytes_accessed=units * 2 * pairs * cols * cols * 2,
            transcendentals=0,
        ),
        name=f"sums_{units}",
    )(*near, *away)


UNROLL = 6


def terms_kernel(slots_ref, rows_ref, sizes_ref, right_ref, acc, far_near, far_away, far_ref, left_ref, *refs):
    keep_ref, send_ref, part, total = refs
    _, xh, core, xl, y = position()
    arrays = (far_near, far_away)
    group, cols = far_near.shape[2:]
    pairs = far_ref.shape[2]
    lane = lax.broadcasted_iota(jnp.int32, (1, BLK), 1)
    start = (xl * NY + y) * (cols // BLK)
    live = jnp.concatenate(
        [(lane < right_ref[start + i]).astype(jnp.float32) for i in range(cols // BLK)], axis=1
    )
    height = total.shape[0]
    total[...] = jnp.zeros_like(total)
    for pair in range(2 * pairs):
        for q in range(NZ * NXH):
            at = pl.multiple_of(pair * height + (q * NC + 1 - core) * group, 16)
            part[pl.ds(at, group), :] = jnp.zeros((group, cols), part.dtype)

    def place(half, side, values):
        for pair in range(pairs):
            rounded = (values[:, pair * cols : (pair + 1) * cols] * live).astype(part.dtype)
            for dz in range(NZ):
                at = (side * pairs + pair) * height + ((dz * NXH + half) * NC + core) * group
                part[pl.ds(pl.multiple_of(at, 16), group), :] = rounded[dz * group : (dz + 1) * group]

    @pl.loop(0, 2)
    def _(side):
        @pl.when(core == 0)
        def _():
            far = 1 - xh
            place(xh, side, acc[xh, side])
            left_side = jnp.concatenate([wide(array) for array in arrays], axis=1)
            right_side = jnp.concatenate([operator(far_ref, i, side) for i in range(2)], axis=1)
            place(far, side, acc[far, side] + times(left_side, right_side))

        @pl.when(core == 1)
        def _():
            for index, (array, half) in enumerate(zip(arrays, (xh, 1 - xh))):
                place(half, side, acc[half, side] + times(wide(array), operator(far_ref, index, side)))

    last_block = 2 * pairs * height // BLK - 1

    @pl.loop(0, rows_ref.shape[0] // UNROLL)
    def _(step):
        for turn in range(UNROLL):
            number = step * UNROLL + turn
            slots = [slots_ref[2 * number + way] for way in range(2)]
            blocks = [jnp.minimum(slot // 2, last_block) for slot in slots]
            result = jnp.dot(
                jnp.concatenate([left_ref[slot] for slot in slots], axis=1),
                jnp.concatenate(
                    [part[pl.ds(pl.multiple_of(block * BLK, BLK), BLK), :] for block in blocks], axis=0
                ),
                preferred_element_type=jnp.float32,
            )
            total[pl.ds(pl.multiple_of(rows_ref[number] * BLK, BLK), BLK), :] += result

    for q in range(NZ * NXH):
        mine = pl.multiple_of((q * NC + core) * group, 16)
        theirs = pl.multiple_of((q * NC + 1 - core) * group, 16)
        keep_ref[q] = jnp.where(row_live(mine, sizes_ref, group), total[pl.ds(mine, group), :], 0.0)
        other = jnp.where(row_live(theirs, sizes_ref, group), total[pl.ds(theirs, group), :], 0.0)
        send_ref[q] = other.astype(send_ref.dtype)


def terms(slots, rows, left_sizes, right_sizes, acc, far_near, far_away, far, left):
    group, cols = far_near.shape[2:]
    height = NZ * NXH * NC * group
    pairs = 2 * far.shape[2]
    assert rows.shape[0] % UNROLL == 0
    return pl.pallas_call(
        terms_kernel,
        out_shape=(
            jax.ShapeDtypeStruct((NZ * NXH, group, cols), jnp.float32),
            jax.ShapeDtypeStruct((NZ * NXH, group, cols), jnp.bfloat16),
        ),
        in_specs=[SMEM_SPEC] * 4 + [VMEM_SPEC] * 5,
        out_specs=(VMEM_SPEC, VMEM_SPEC),
        scratch_shapes=[
            pltpu.VMEM((pairs * height, cols), jnp.bfloat16),
            pltpu.VMEM((height, cols), jnp.float32),
        ],
        compiler_params=pltpu.CompilerParams(vmem_limit_bytes=VMEM_LIMIT),
        name="terms",
    )(slots, rows, left_sizes, right_sizes, acc, far_near, far_away, far, left)


def local(psi, left_ops, a_rows, right_ops, left_sizes, right_sizes):
    copies = mask_psi(left_sizes, right_sizes, psi)
    right = (right_ops, core_swap(right_ops))
    flat_left = left_ops.reshape((-1, BLK, BLK))
    left = (flat_left, core_swap(flat_left))
    rows_by_slot = jnp.transpose(a_rows, (0, 2, 1))
    slots, rows = plan(rows_by_slot, core_swap(rows_by_slot))

    along_z = exchange(copies, z_groups())
    beside = partner(along_z, "middle", 1)
    across = partner(along_z, "middle", 3)
    beside, slots, rows = lax.optimization_barrier((beside, slots, rows))
    near = jnp.stack([along_z, beside])
    near_1 = partner(near, "last", 1)
    near_3 = partner(near, "last", 3)
    away = jnp.stack([across, partner(across, "middle", 1)])
    away_1 = partner(away, "last", 1)
    away_3 = partner(away, "last", 3)
    acc, both = sums(None, [(near, 0, NEAR), (away, 0, AWAY)], right, left)
    near_3, away_1, acc = lax.optimization_barrier((near_3, away_1, acc))
    near_2 = partner(near_3, "last", 1)
    away_2 = partner(away_1, "last", 3)
    acc, far = sums(
        acc,
        [(near_1, 1, NEAR), (near_3, 3, NEAR), (away_1, 1, AWAY), (away_3, 3, AWAY)],
        right,
        ahead=((2, NEAR), (2, AWAY)),
    )
    keep, send = terms(slots, rows, left_sizes, right_sizes, acc, near_2, away_2, far, both)
    mine = (keep + core_swap(send).astype(jnp.float32)).astype(jnp.bfloat16)
    groups = [
        [flat(z, xh * NXL + xl, y, c) for z in range(NZ) for xh in range(NXH)]
        for c in range(NC)
        for xl in range(NXL)
        for y in range(NY)
    ]
    parts = exchange(mine, groups)
    return parts.astype(jnp.float32).sum(axis=0)


def solution(mesh):
    placed = (
        P("pair", "panel"),
        P("pair", None, None, None, None),
        P("pair", None, None),
        P("pair", "panel", None),
        P(),
        P(),
    )
    return jax.shard_map(
        local, mesh=mesh, in_specs=placed, out_specs=P("pair", "panel"), check_vma=False
    )
```

```python
import functools

import jax
import jax.numpy as jnp
from jax import lax
from jax.experimental import pallas as pl
from jax.experimental.pallas import tpu as pltpu
from jax.sharding import PartitionSpec as P

BLK = 128
NZ, NXH, NC, NXL, NY = 8, 2, 2, 2, 4
NX = NXH * NXL
AXES = ("pair", "panel")
VMEM_LIMIT = 28 * 1024 * 1024
SMALL_LIMIT = 2 * 1024 * 1024
SMEM_SPEC = pl.BlockSpec(memory_space=pltpu.SMEM)
VMEM_SPEC = pl.BlockSpec(memory_space=pltpu.VMEM)
HBM_SPEC = pl.BlockSpec(memory_space=pltpu.HBM)


def flat(z, x, y, core):
    pair = (z * NXH + x // NXL) * NC + core
    return pair * (NXL * NY) + (x % NXL) * NY + y


def everywhere():
    return [
        (z, x, y, core) for z in range(NZ) for x in range(NX) for y in range(NY) for core in range(NC)
    ]


def core_swap(value):
    return lax.ppermute(
        value, AXES, [(flat(z, x, y, 1 - c), flat(z, x, y, c)) for z, x, y, c in everywhere()]
    )


def partner(value, ring, step):
    perm = []
    for z, x, y, c in everywhere():
        along_x = (ring == "last") == (c == 0)
        source = flat(z, x ^ step, y, c) if along_x else flat(z, x, y ^ step, c)
        perm.append((source, flat(z, x, y, c)))
    return lax.ppermute(value, AXES, perm)


def exchange(copies, groups):
    return lax.all_to_all(
        copies, AXES, split_axis=0, concat_axis=0, axis_index_groups=groups, tiled=True
    )


def z_groups():
    return [
        [flat(z, x, y, c) for z in range(NZ)] for x in range(NX) for y in range(NY) for c in range(NC)
    ]


def position():
    pair, panel = lax.axis_index("pair"), lax.axis_index("panel")
    return pair // (NXH * NC), (pair // NC) % NXH, pair % NC, panel // NY, panel % NY


def row_live(base, left_ref, count):
    first = base // BLK
    second = jnp.minimum(first + 1, left_ref.shape[0] - 1)
    index = base + lax.broadcasted_iota(jnp.int32, (count, 1), 0)
    end = (first + 1) * BLK
    return index < jnp.where(index < end, first * BLK + left_ref[first], end + left_ref[second])


def mask_kernel(left_ref, right_ref, psi_ref, out_ref):
    rows, cols = psi_ref.shape
    panel = lax.axis_index("panel")
    rows_live = row_live(lax.axis_index("pair") * rows, left_ref, rows)
    lane = lax.broadcasted_iota(jnp.int32, (rows, BLK), 1)
    for block in range(cols // BLK):
        live = rows_live & (lane < right_ref[panel * (cols // BLK) + block])
        span = slice(block * BLK, (block + 1) * BLK)
        value = psi_ref[:, span].astype(jnp.float32)
        value = jnp.where(live, value, 0.0).astype(out_ref.dtype)
        for copy in range(out_ref.shape[0]):
            out_ref[copy, :, span] = value


def mask_psi(left_sizes, right_sizes, psi):
    return pl.pallas_call(
        mask_kernel,
        out_shape=jax.ShapeDtypeStruct((NZ,) + psi.shape, psi.dtype),
        in_specs=[SMEM_SPEC, SMEM_SPEC, VMEM_SPEC],
        out_specs=VMEM_SPEC,
        name="mask_psi",
    )(left_sizes, right_sizes, psi)


def plan_kernel(own_ref, other_ref, slots_ref, rows_ref, next_ref):
    shape = own_ref.shape
    count = own_ref.size
    slots = [
        (side, pair, block, s)
        for side in range(2)
        for pair in range(shape[0])
        for block in range(shape[2])
        for s in range(shape[1])
    ]

    def row_of(slot):
        return (own_ref, other_ref)[slot[0]][slot[1], slot[3], slot[2]]

    for place in range(slots_ref.shape[0]):
        slots_ref[place] = 2 * count
    for place in range(rows_ref.shape[0]):
        rows_ref[place] = 0
    for row in range(shape[2]):
        next_ref[row] = 0
    for slot in slots:
        row = row_of(slot)
        next_ref[row] = next_ref[row] + 1
    start = jnp.int32(0)
    for row in range(shape[2]):
        pairs = (next_ref[row] + 1) // 2
        next_ref[row] = 2 * start

        @pl.loop(0, pairs)
        def _(i):
            rows_ref[start + i] = row

        start = start + pairs
    for number, slot in enumerate(slots):
        row = row_of(slot)
        place = next_ref[row]
        slots_ref[place] = number
        next_ref[row] = place + 1


def plan(own, other):
    pairs = own.size + own.shape[2] // 2
    return pl.pallas_call(
        plan_kernel,
        out_shape=(
            jax.ShapeDtypeStruct((2 * pairs,), jnp.int32),
            jax.ShapeDtypeStruct((pairs,), jnp.int32),
        ),
        in_specs=[SMEM_SPEC, SMEM_SPEC],
        out_specs=(SMEM_SPEC, SMEM_SPEC),
        scratch_shapes=[pltpu.SMEM((own.shape[2],), jnp.int32)],
        compiler_params=pltpu.CompilerParams(vmem_limit_bytes=SMALL_LIMIT),
        name="plan",
    )(own, other)


NEAR, AWAY = (0, 1), (3, 2)


def two_copies(twos, right, buffer, sem):
    _, xh, core, xl, y = position()
    x = xh * NXL + xl
    cols = right[0].shape[1]
    copies, halves = [], []
    for index, (step, places) in enumerate(twos):
        copies.append([])
        for way, place in enumerate(places):
            unit_x = jnp.where(core == 0, x ^ step, x ^ place)
            unit_y = jnp.where(core == 0, y ^ place, y ^ step)
            column = pl.multiple_of((lax.rem(unit_x, NXL) * NY + unit_y) * cols, BLK)
            for side in range(2):
                copies[-1].append(
                    pltpu.make_async_copy(
                        right[side].at[:, :, pl.ds(column, cols)],
                        buffer.at[index, side, :, :, pl.ds(way * cols, cols)],
                        sem.at[index, side, way],
                    )
                )
        halves.append(unit_x // NXL)
    return copies, halves


def wide(array):
    rows = array.shape[1] * array.shape[2]
    return jnp.concatenate([array[way].reshape(rows, array.shape[3]) for way in range(2)], axis=1)


def times(left_side, right_side):
    return lax.dot_general(
        left_side, right_side, (((1,), (1,)), ((), ())), preferred_element_type=jnp.float32
    )


def operator(buffer, index, side):
    return buffer[index, side].reshape(buffer.shape[2] * buffer.shape[3], buffer.shape[4])


def sums_kernel(twos, first, ahead, *refs):
    refs = list(refs)
    acc_in = None if first else refs.pop(0)
    arrays = [refs.pop(0) for _ in twos]
    right = (refs.pop(0), refs.pop(0))
    left = (refs.pop(0), refs.pop(0)) if first else None
    acc = refs.pop(0)
    later_ref = refs.pop(0) if first or ahead else None
    rbuf, sem, later_sem = refs
    copies, halves = two_copies(twos, right, rbuf, sem)
    later = []
    if ahead:
        later = sum(two_copies(ahead, right, later_ref, later_sem)[0], [])
    if first:
        count = left[0].shape[0]
        later = [
            pltpu.make_async_copy(
                left[side], later_ref.at[pl.ds(side * count, count)], later_sem.at[side]
            )
            for side in range(2)
        ]
        later_ref[2 * count] = jnp.zeros(later_ref.shape[1:], later_ref.dtype)
    for copy in sum(copies, []) + later:
        copy.start()
    acc[...] = jnp.zeros_like(acc) if first else acc_in[...]
    for index, array in enumerate(arrays):
        for copy in copies[index]:
            copy.wait()

        @pl.loop(0, 2)
        def _(side):
            acc[halves[index], side] += times(wide(array), operator(rbuf, index, side))

    for copy in later:
        copy.wait()


def sums(acc, pieces, right, left=None, ahead=()):
    arrays = [array for array, _, _ in pieces]
    twos = tuple((step, places) for _, step, places in pieces)
    group, cols = arrays[0].shape[2:]
    pairs = right[0].shape[0]
    units = 2 * len(arrays)
    first = acc is None
    near, away = ([] if first else [acc]) + arrays, list(right) + (list(left) if first else [])
    out_shape = [jax.ShapeDtypeStruct((NXH, 2, NZ * group, pairs * cols), jnp.float32)]
    if first:
        later = (2 * left[0].shape[0] + 1,) + left[0].shape[1:]
        out_shape.append(jax.ShapeDtypeStruct(later, jnp.bfloat16))
    if ahead:
        out_shape.append(jax.ShapeDtypeStruct((2, 2, pairs, cols, 2 * cols), jnp.bfloat16))
    return pl.pallas_call(
        functools.partial(sums_kernel, twos, first, ahead),
        out_shape=out_shape,
        in_specs=[VMEM_SPEC] * len(near) + [HBM_SPEC] * len(away),
        out_specs=[VMEM_SPEC] * len(out_shape),
        scratch_shapes=[
            pltpu.VMEM((units // 2, 2, pairs, cols, 2 * cols), jnp.bfloat16),
            pltpu.SemaphoreType.DMA((units // 2, 2, 2)),
            pltpu.SemaphoreType.DMA((2, 2, 2) if ahead else (2,)),
        ],
        input_output_aliases={} if first else {0: 0},
        compiler_params=pltpu.CompilerParams(vmem_limit_bytes=VMEM_LIMIT),
        cost_estimate=pl.CostEstimate(
            flops=2 * units * 2 * pairs * NZ * group * cols * cols,
            bytes_accessed=units * 2 * pairs * cols * cols * 2,
            transcendentals=0,
        ),
        name=f"sums_{'first' if first else 'last' if ahead else 'middle'}",
    )(*near, *away)


UNROLL = 6


def terms_kernel(slots_ref, rows_ref, sizes_ref, right_ref, acc, far_near, far_away, far_ref, left_ref, *refs):
    keep_ref, send_ref, part, total = refs
    _, xh, core, xl, y = position()
    arrays = (far_near, far_away)
    group, cols = far_near.shape[2:]
    pairs = far_ref.shape[2]
    lane = lax.broadcasted_iota(jnp.int32, (1, BLK), 1)
    start = (xl * NY + y) * (cols // BLK)
    live = jnp.concatenate(
        [(lane < right_ref[start + i]).astype(jnp.float32) for i in range(cols // BLK)], axis=1
    )
    height = total.shape[0]
    total[...] = jnp.zeros_like(total)
    for pair in range(2 * pairs):
        for q in range(NZ * NXH):
            at = pl.multiple_of(pair * height + (q * NC + 1 - core) * group, 16)
            part[pl.ds(at, group), :] = jnp.zeros((group, cols), part.dtype)

    def place(half, side, values):
        for pair in range(pairs):
            rounded = (values[:, pair * cols : (pair + 1) * cols] * live).astype(part.dtype)
            for dz in range(NZ):
                at = (side * pairs + pair) * height + ((dz * NXH + half) * NC + core) * group
                part[pl.ds(pl.multiple_of(at, 16), group), :] = rounded[dz * group : (dz + 1) * group]

    @pl.loop(0, 2)
    def _(side):
        @pl.when(core == 0)
        def _():
            far = 1 - xh
            place(xh, side, acc[xh, side])
            left_side = jnp.concatenate([wide(array) for array in arrays], axis=1)
            right_side = jnp.concatenate([operator(far_ref, i, side) for i in range(2)], axis=1)
            place(far, side, acc[far, side] + times(left_side, right_side))

        @pl.when(core == 1)
        def _():
            for index, (array, half) in enumerate(zip(arrays, (xh, 1 - xh))):
                place(half, side, acc[half, side] + times(wide(array), operator(far_ref, index, side)))

    last_block = 2 * pairs * height // BLK - 1

    @pl.loop(0, rows_ref.shape[0] // UNROLL)
    def _(step):
        for turn in range(UNROLL):
            number = step * UNROLL + turn
            slots = [slots_ref[2 * number + way] for way in range(2)]
            blocks = [jnp.minimum(slot // 2, last_block) for slot in slots]
            result = jnp.dot(
                jnp.concatenate([left_ref[slot] for slot in slots], axis=1),
                jnp.concatenate(
                    [part[pl.ds(pl.multiple_of(block * BLK, BLK), BLK), :] for block in blocks], axis=0
                ),
                preferred_element_type=jnp.float32,
            )
            total[pl.ds(pl.multiple_of(rows_ref[number] * BLK, BLK), BLK), :] += result

    for q in range(NZ * NXH):
        mine = pl.multiple_of((q * NC + core) * group, 16)
        theirs = pl.multiple_of((q * NC + 1 - core) * group, 16)
        keep_ref[q] = jnp.where(row_live(mine, sizes_ref, group), total[pl.ds(mine, group), :], 0.0)
        other = jnp.where(row_live(theirs, sizes_ref, group), total[pl.ds(theirs, group), :], 0.0)
        send_ref[q] = other.astype(send_ref.dtype)


def terms(slots, rows, left_sizes, right_sizes, acc, far_near, far_away, far, left):
    group, cols = far_near.shape[2:]
    height = NZ * NXH * NC * group
    pairs = 2 * far.shape[2]
    assert rows.shape[0] % UNROLL == 0
    return pl.pallas_call(
        terms_kernel,
        out_shape=(
            jax.ShapeDtypeStruct((NZ * NXH, group, cols), jnp.float32),
            jax.ShapeDtypeStruct((NZ * NXH, group, cols), jnp.bfloat16),
        ),
        in_specs=[SMEM_SPEC] * 4 + [VMEM_SPEC] * 5,
        out_specs=(VMEM_SPEC, VMEM_SPEC),
        scratch_shapes=[
            pltpu.VMEM((pairs * height, cols), jnp.bfloat16),
            pltpu.VMEM((height, cols), jnp.float32),
        ],
        compiler_params=pltpu.CompilerParams(vmem_limit_bytes=VMEM_LIMIT),
        name="terms",
    )(slots, rows, left_sizes, right_sizes, acc, far_near, far_away, far, left)


def local(psi, left_ops, a_rows, right_ops, left_sizes, right_sizes):
    copies = mask_psi(left_sizes, right_sizes, psi)
    right = (right_ops, core_swap(right_ops))
    flat_left = left_ops.reshape((-1, BLK, BLK))
    left = (flat_left, core_swap(flat_left))
    rows_by_slot = jnp.transpose(a_rows, (0, 2, 1))
    rows_other = core_swap(rows_by_slot)

    along_z = exchange(copies, z_groups())
    beside = partner(along_z, "middle", 1)
    across = partner(along_z, "middle", 3)
    near = jnp.stack([along_z, beside])
    near_1 = partner(near, "last", 1)
    near_3 = partner(near, "last", 3)
    away = jnp.stack([across, partner(across, "middle", 1)])
    away_1 = partner(away, "last", 1)
    away_3 = partner(away, "last", 3)
    acc, both = sums(None, [(near, 0, NEAR), (away, 0, AWAY)], right, left)
    (acc,) = sums(acc, [(near_1, 1, NEAR), (near_3, 3, NEAR)], right)
    near_3, away_1, acc = lax.optimization_barrier((near_3, away_1, acc))
    near_2 = partner(near_3, "last", 1)
    away_2 = partner(away_1, "last", 3)
    acc, far = sums(
        acc, [(away_1, 1, AWAY), (away_3, 3, AWAY)], right, ahead=((2, NEAR), (2, AWAY))
    )
    rows_other, acc = lax.optimization_barrier((rows_other, acc))
    slots, rows = plan(rows_by_slot, rows_other)
    keep, send = terms(slots, rows, left_sizes, right_sizes, acc, near_2, away_2, far, both)
    mine = (keep + core_swap(send).astype(jnp.float32)).astype(jnp.bfloat16)
    groups = [
        [flat(z, xh * NXL + xl, y, c) for z in range(NZ) for xh in range(NXH)]
        for c in range(NC)
        for xl in range(NXL)
        for y in range(NY)
    ]
    parts = exchange(mine, groups)
    return parts.astype(jnp.float32).sum(axis=0)


def solution(mesh):
    placed = (
        P("pair", "panel"),
        P("pair", None, None, None, None),
        P("pair", None, None),
        P("pair", "panel", None),
        P(),
        P(),
    )
    return jax.shard_map(
        local, mesh=mesh, in_specs=placed, out_specs=P("pair", "panel"), check_vma=False
    )
```

```python
import functools

import jax
import jax.numpy as jnp
from jax import lax
from jax.experimental import pallas as pl
from jax.experimental.pallas import tpu as pltpu
from jax.sharding import PartitionSpec as P

BLK = 128
NZ, NXH, NC, NXL, NY = 8, 2, 2, 2, 4
NX = NXH * NXL
AXES = ("pair", "panel")
VMEM_LIMIT = 28 * 1024 * 1024
SMALL_LIMIT = 2 * 1024 * 1024
SMEM_SPEC = pl.BlockSpec(memory_space=pltpu.SMEM)
VMEM_SPEC = pl.BlockSpec(memory_space=pltpu.VMEM)
HBM_SPEC = pl.BlockSpec(memory_space=pltpu.HBM)


def flat(z, x, y, core):
    pair = (z * NXH + x // NXL) * NC + core
    return pair * (NXL * NY) + (x % NXL) * NY + y


def everywhere():
    return [
        (z, x, y, core) for z in range(NZ) for x in range(NX) for y in range(NY) for core in range(NC)
    ]


def core_swap(value):
    return lax.ppermute(
        value, AXES, [(flat(z, x, y, 1 - c), flat(z, x, y, c)) for z, x, y, c in everywhere()]
    )


def partner(value, ring, step):
    perm = []
    for z, x, y, c in everywhere():
        along_x = (ring == "last") == (c == 0)
        source = flat(z, x ^ step, y, c) if along_x else flat(z, x, y ^ step, c)
        perm.append((source, flat(z, x, y, c)))
    return lax.ppermute(value, AXES, perm)


def exchange(copies, groups):
    return lax.all_to_all(
        copies, AXES, split_axis=0, concat_axis=0, axis_index_groups=groups, tiled=True
    )


def z_groups():
    return [
        [flat(z, x, y, c) for z in range(NZ)] for x in range(NX) for y in range(NY) for c in range(NC)
    ]


def position():
    pair, panel = lax.axis_index("pair"), lax.axis_index("panel")
    return pair // (NXH * NC), (pair // NC) % NXH, pair % NC, panel // NY, panel % NY


def row_live(base, left_ref, count):
    first = base // BLK
    second = jnp.minimum(first + 1, left_ref.shape[0] - 1)
    index = base + lax.broadcasted_iota(jnp.int32, (count, 1), 0)
    end = (first + 1) * BLK
    return index < jnp.where(index < end, first * BLK + left_ref[first], end + left_ref[second])


def mask_kernel(left_ref, right_ref, psi_ref, out_ref):
    rows, cols = psi_ref.shape
    panel = lax.axis_index("panel")
    rows_live = row_live(lax.axis_index("pair") * rows, left_ref, rows)
    lane = lax.broadcasted_iota(jnp.int32, (rows, BLK), 1)
    for block in range(cols // BLK):
        live = rows_live & (lane < right_ref[panel * (cols // BLK) + block])
        span = slice(block * BLK, (block + 1) * BLK)
        value = psi_ref[:, span].astype(jnp.float32)
        value = jnp.where(live, value, 0.0).astype(out_ref.dtype)
        for copy in range(out_ref.shape[0]):
            out_ref[copy, :, span] = value


def mask_psi(left_sizes, right_sizes, psi):
    return pl.pallas_call(
        mask_kernel,
        out_shape=jax.ShapeDtypeStruct((NZ,) + psi.shape, psi.dtype),
        in_specs=[SMEM_SPEC, SMEM_SPEC, VMEM_SPEC],
        out_specs=VMEM_SPEC,
        name="mask_psi",
    )(left_sizes, right_sizes, psi)


def plan_kernel(own_ref, other_ref, slots_ref, rows_ref, next_ref):
    shape = own_ref.shape
    count = own_ref.size
    slots = [
        (side, pair, block, s)
        for side in range(2)
        for pair in range(shape[0])
        for block in range(shape[2])
        for s in range(shape[1])
    ]

    def row_of(slot):
        return (own_ref, other_ref)[slot[0]][slot[1], slot[3], slot[2]]

    for place in range(slots_ref.shape[0]):
        slots_ref[place] = 2 * count
    for place in range(rows_ref.shape[0]):
        rows_ref[place] = 0
    for row in range(shape[2]):
        next_ref[row] = 0
    for slot in slots:
        row = row_of(slot)
        next_ref[row] = next_ref[row] + 1
    start = jnp.int32(0)
    for row in range(shape[2]):
        pairs = (next_ref[row] + 1) // 2
        next_ref[row] = 2 * start

        @pl.loop(0, pairs)
        def _(i):
            rows_ref[start + i] = row

        start = start + pairs
    for number, slot in enumerate(slots):
        row = row_of(slot)
        place = next_ref[row]
        slots_ref[place] = number
        next_ref[row] = place + 1


def plan(own, other):
    pairs = own.size + own.shape[2] // 2
    return pl.pallas_call(
        plan_kernel,
        out_shape=(
            jax.ShapeDtypeStruct((2 * pairs,), jnp.int32),
            jax.ShapeDtypeStruct((pairs,), jnp.int32),
        ),
        in_specs=[SMEM_SPEC, SMEM_SPEC],
        out_specs=(SMEM_SPEC, SMEM_SPEC),
        scratch_shapes=[pltpu.SMEM((own.shape[2],), jnp.int32)],
        compiler_params=pltpu.CompilerParams(vmem_limit_bytes=SMALL_LIMIT),
        name="plan",
    )(own, other)


NEAR, AWAY = (0, 1), (3, 2)


def two_copies(twos, right, buffer, sem):
    _, xh, core, xl, y = position()
    x = xh * NXL + xl
    cols = right[0].shape[1]
    copies, halves = [], []
    for index, (step, places) in enumerate(twos):
        copies.append([])
        for way, place in enumerate(places):
            unit_x = jnp.where(core == 0, x ^ step, x ^ place)
            unit_y = jnp.where(core == 0, y ^ place, y ^ step)
            column = pl.multiple_of((lax.rem(unit_x, NXL) * NY + unit_y) * cols, BLK)
            for side in range(2):
                copies[-1].append(
                    pltpu.make_async_copy(
                        right[side].at[:, :, pl.ds(column, cols)],
                        buffer.at[index, side, :, :, pl.ds(way * cols, cols)],
                        sem.at[index, side, way],
                    )
                )
        halves.append(unit_x // NXL)
    return copies, halves


def wide(array):
    rows = array.shape[1] * array.shape[2]
    return jnp.concatenate([array[way].reshape(rows, array.shape[3]) for way in range(2)], axis=1)


def times(left_side, right_side):
    return lax.dot_general(
        left_side, right_side, (((1,), (1,)), ((), ())), preferred_element_type=jnp.float32
    )


def operator(buffer, index, side):
    return buffer[index, side].reshape(buffer.shape[2] * buffer.shape[3], buffer.shape[4])


def sums_kernel(twos, first, ahead, *refs):
    refs = list(refs)
    acc_in = None if first else refs.pop(0)
    arrays = [refs.pop(0) for _ in twos]
    right = (refs.pop(0), refs.pop(0))
    left = (refs.pop(0), refs.pop(0)) if first else None
    acc = refs.pop(0)
    later_ref = refs.pop(0) if first or ahead else None
    rbuf, sem, later_sem = refs
    copies, halves = two_copies(twos, right, rbuf, sem)
    later = []
    if ahead:
        later = sum(two_copies(ahead, right, later_ref, later_sem)[0], [])
    if first:
        count = left[0].shape[0]
        later = [
            pltpu.make_async_copy(
                left[side], later_ref.at[pl.ds(side * count, count)], later_sem.at[side]
            )
            for side in range(2)
        ]
        later_ref[2 * count] = jnp.zeros(later_ref.shape[1:], later_ref.dtype)
    for copy in sum(copies, []) + later:
        copy.start()
    acc[...] = jnp.zeros_like(acc) if first else acc_in[...]
    for index, array in enumerate(arrays):
        for copy in copies[index]:
            copy.wait()

        @pl.loop(0, 2)
        def _(side):
            acc[halves[index], side] += times(wide(array), operator(rbuf, index, side))

    for copy in later:
        copy.wait()


def sums(acc, pieces, right, left=None, ahead=()):
    arrays = [array for array, _, _ in pieces]
    twos = tuple((step, places) for _, step, places in pieces)
    group, cols = arrays[0].shape[2:]
    pairs = right[0].shape[0]
    units = 2 * len(arrays)
    first = acc is None
    near, away = ([] if first else [acc]) + arrays, list(right) + (list(left) if first else [])
    out_shape = [jax.ShapeDtypeStruct((NXH, 2, NZ * group, pairs * cols), jnp.float32)]
    if first:
        later = (2 * left[0].shape[0] + 1,) + left[0].shape[1:]
        out_shape.append(jax.ShapeDtypeStruct(later, jnp.bfloat16))
    if ahead:
        out_shape.append(jax.ShapeDtypeStruct((2, 2, pairs, cols, 2 * cols), jnp.bfloat16))
    return pl.pallas_call(
        functools.partial(sums_kernel, twos, first, ahead),
        out_shape=out_shape,
        in_specs=[VMEM_SPEC] * len(near) + [HBM_SPEC] * len(away),
        out_specs=[VMEM_SPEC] * len(out_shape),
        scratch_shapes=[
            pltpu.VMEM((units // 2, 2, pairs, cols, 2 * cols), jnp.bfloat16),
            pltpu.SemaphoreType.DMA((units // 2, 2, 2)),
            pltpu.SemaphoreType.DMA((2, 2, 2) if ahead else (2,)),
        ],
        input_output_aliases={} if first else {0: 0},
        compiler_params=pltpu.CompilerParams(vmem_limit_bytes=VMEM_LIMIT),
        cost_estimate=pl.CostEstimate(
            flops=2 * units * 2 * pairs * NZ * group * cols * cols,
            bytes_accessed=units * 2 * pairs * cols * cols * 2,
            transcendentals=0,
        ),
        name=f"sums_{'first' if first else 'last' if ahead else 'middle'}",
    )(*near, *away)


UNROLL = 6


def terms_kernel(slots_ref, rows_ref, sizes_ref, right_ref, acc, far_near, far_away, far_ref, left_ref, *refs):
    keep_ref, send_ref, part, total = refs
    _, xh, core, xl, y = position()
    arrays = (far_near, far_away)
    group, cols = far_near.shape[2:]
    pairs = far_ref.shape[2]
    lane = lax.broadcasted_iota(jnp.int32, (1, BLK), 1)
    start = (xl * NY + y) * (cols // BLK)
    live = jnp.concatenate(
        [(lane < right_ref[start + i]).astype(jnp.float32) for i in range(cols // BLK)], axis=1
    )
    height = total.shape[0]
    total[...] = jnp.zeros_like(total)
    for pair in range(2 * pairs):
        for q in range(NZ * NXH):
            at = pl.multiple_of(pair * height + (q * NC + 1 - core) * group, 16)
            part[pl.ds(at, group), :] = jnp.zeros((group, cols), part.dtype)

    def place(half, side, values):
        for pair in range(pairs):
            rounded = (values[:, pair * cols : (pair + 1) * cols] * live).astype(part.dtype)
            for dz in range(NZ):
                at = (side * pairs + pair) * height + ((dz * NXH + half) * NC + core) * group
                part[pl.ds(pl.multiple_of(at, 16), group), :] = rounded[dz * group : (dz + 1) * group]

    @pl.loop(0, 2)
    def _(side):
        @pl.when(core == 0)
        def _():
            far = 1 - xh
            place(xh, side, acc[xh, side])
            left_side = jnp.concatenate([wide(array) for array in arrays], axis=1)
            right_side = jnp.concatenate([operator(far_ref, i, side) for i in range(2)], axis=1)
            place(far, side, acc[far, side] + times(left_side, right_side))

        @pl.when(core == 1)
        def _():
            for index, (array, half) in enumerate(zip(arrays, (xh, 1 - xh))):
                place(half, side, acc[half, side] + times(wide(array), operator(far_ref, index, side)))

    last_block = 2 * pairs * height // BLK - 1

    @pl.loop(0, rows_ref.shape[0] // UNROLL)
    def _(step):
        for turn in range(UNROLL):
            number = step * UNROLL + turn
            slots = [slots_ref[2 * number + way] for way in range(2)]
            blocks = [jnp.minimum(slot // 2, last_block) for slot in slots]
            result = jnp.dot(
                jnp.concatenate([left_ref[slot] for slot in slots], axis=1),
                jnp.concatenate(
                    [part[pl.ds(pl.multiple_of(block * BLK, BLK), BLK), :] for block in blocks], axis=0
                ),
                preferred_element_type=jnp.float32,
            )
            total[pl.ds(pl.multiple_of(rows_ref[number] * BLK, BLK), BLK), :] += result

    for q in range(NZ * NXH):
        mine = pl.multiple_of((q * NC + core) * group, 16)
        theirs = pl.multiple_of((q * NC + 1 - core) * group, 16)
        keep_ref[q] = jnp.where(row_live(mine, sizes_ref, group), total[pl.ds(mine, group), :], 0.0)
        other = jnp.where(row_live(theirs, sizes_ref, group), total[pl.ds(theirs, group), :], 0.0)
        send_ref[q] = other.astype(send_ref.dtype)


def terms(slots, rows, left_sizes, right_sizes, acc, far_near, far_away, far, left):
    group, cols = far_near.shape[2:]
    height = NZ * NXH * NC * group
    pairs = 2 * far.shape[2]
    assert rows.shape[0] % UNROLL == 0
    return pl.pallas_call(
        terms_kernel,
        out_shape=(
            jax.ShapeDtypeStruct((NZ * NXH, group, cols), jnp.float32),
            jax.ShapeDtypeStruct((NZ * NXH, group, cols), jnp.bfloat16),
        ),
        in_specs=[SMEM_SPEC] * 4 + [VMEM_SPEC] * 5,
        out_specs=(VMEM_SPEC, VMEM_SPEC),
        scratch_shapes=[
            pltpu.VMEM((pairs * height, cols), jnp.bfloat16),
            pltpu.VMEM((height, cols), jnp.float32),
        ],
        compiler_params=pltpu.CompilerParams(vmem_limit_bytes=VMEM_LIMIT),
        name="terms",
    )(slots, rows, left_sizes, right_sizes, acc, far_near, far_away, far, left)


def local(psi, left_ops, a_rows, right_ops, left_sizes, right_sizes):
    copies = mask_psi(left_sizes, right_sizes, psi)
    right = (right_ops, core_swap(right_ops))
    flat_left = left_ops.reshape((-1, BLK, BLK))
    left = (flat_left, core_swap(flat_left))
    rows_by_slot = jnp.transpose(a_rows, (0, 2, 1))
    rows_other = core_swap(rows_by_slot)

    along_z = exchange(copies, z_groups())
    beside = partner(along_z, "middle", 1)
    across = partner(along_z, "middle", 3)
    opposite = partner(across, "middle", 1)
    near, away = jnp.stack([along_z, beside]), jnp.stack([across, opposite])
    near, away, rows_other = lax.optimization_barrier((near, away, rows_other))
    near_3 = partner(near, "last", 3)
    away_1 = partner(away, "last", 1)
    near_1 = partner(near, "last", 1)
    away_3 = partner(away, "last", 3)
    slots, rows = plan(rows_by_slot, rows_other)
    near, slots, rows = lax.optimization_barrier((near, slots, rows))
    acc, both = sums(None, [(near, 0, NEAR), (away, 0, AWAY)], right, left)
    near_3, away_1, acc = lax.optimization_barrier((near_3, away_1, acc))
    near_2 = partner(near_3, "last", 1)
    away_2 = partner(away_1, "last", 3)
    (acc,) = sums(acc, [(near_3, 3, NEAR), (away_1, 1, AWAY)], right)
    acc, far = sums(
        acc, [(near_1, 1, NEAR), (away_3, 3, AWAY)], right, ahead=((2, NEAR), (2, AWAY))
    )
    keep, send = terms(slots, rows, left_sizes, right_sizes, acc, near_2, away_2, far, both)
    mine = (keep + core_swap(send).astype(jnp.float32)).astype(jnp.bfloat16)
    groups = [
        [flat(z, xh * NXL + xl, y, c) for z in range(NZ) for xh in range(NXH)]
        for c in range(NC)
        for xl in range(NXL)
        for y in range(NY)
    ]
    parts = exchange(mine, groups)
    return parts.astype(jnp.float32).sum(axis=0)


def solution(mesh):
    placed = (
        P("pair", "panel"),
        P("pair", None, None, None, None),
        P("pair", None, None),
        P("pair", "panel", None),
        P(),
        P(),
    )
    return jax.shard_map(
        local, mesh=mesh, in_specs=placed, out_specs=P("pair", "panel"), check_vma=False
    )
```

```python
import functools

import jax
import jax.numpy as jnp
from jax import lax
from jax.experimental import pallas as pl
from jax.experimental.pallas import tpu as pltpu
from jax.sharding import PartitionSpec as P

BLK = 128
NZ, NXH, NC, NXL, NY = 8, 2, 2, 2, 4
NX = NXH * NXL
AXES = ("pair", "panel")
VMEM_LIMIT = 28 * 1024 * 1024
SMALL_LIMIT = 2 * 1024 * 1024
SMEM_SPEC = pl.BlockSpec(memory_space=pltpu.SMEM)
VMEM_SPEC = pl.BlockSpec(memory_space=pltpu.VMEM)
HBM_SPEC = pl.BlockSpec(memory_space=pltpu.HBM)


def flat(z, x, y, core):
    pair = (z * NXH + x // NXL) * NC + core
    return pair * (NXL * NY) + (x % NXL) * NY + y


def everywhere():
    return [
        (z, x, y, core) for z in range(NZ) for x in range(NX) for y in range(NY) for core in range(NC)
    ]


def core_swap(value):
    return lax.ppermute(
        value, AXES, [(flat(z, x, y, 1 - c), flat(z, x, y, c)) for z, x, y, c in everywhere()]
    )


def partner(value, ring, step):
    perm = []
    for z, x, y, c in everywhere():
        along_x = (ring == "last") == (c == 0)
        source = flat(z, x ^ step, y, c) if along_x else flat(z, x, y ^ step, c)
        perm.append((source, flat(z, x, y, c)))
    return lax.ppermute(value, AXES, perm)


def to_owner(value, step):
    perm = []
    for z, x, y, c in everywhere():
        q = (z * NXH + x // NXL) ^ step
        perm.append((flat(q // NXH, (q % NXH) * NXL + x % NXL, y, c), flat(z, x, y, c)))
    return lax.ppermute(value, AXES, perm)


def exchange(copies, groups):
    return lax.all_to_all(
        copies, AXES, split_axis=0, concat_axis=0, axis_index_groups=groups, tiled=True
    )


def z_groups():
    return [
        [flat(z, x, y, c) for z in range(NZ)] for x in range(NX) for y in range(NY) for c in range(NC)
    ]


def position():
    pair, panel = lax.axis_index("pair"), lax.axis_index("panel")
    return pair // (NXH * NC), (pair // NC) % NXH, pair % NC, panel // NY, panel % NY


def row_live(base, left_ref, count):
    first = base // BLK
    second = jnp.minimum(first + 1, left_ref.shape[0] - 1)
    index = base + lax.broadcasted_iota(jnp.int32, (count, 1), 0)
    end = (first + 1) * BLK
    return index < jnp.where(index < end, first * BLK + left_ref[first], end + left_ref[second])


def mask_kernel(left_ref, right_ref, psi_ref, out_ref):
    rows, cols = psi_ref.shape
    panel = lax.axis_index("panel")
    rows_live = row_live(lax.axis_index("pair") * rows, left_ref, rows)
    lane = lax.broadcasted_iota(jnp.int32, (rows, BLK), 1)
    for block in range(cols // BLK):
        live = rows_live & (lane < right_ref[panel * (cols // BLK) + block])
        span = slice(block * BLK, (block + 1) * BLK)
        value = psi_ref[:, span].astype(jnp.float32)
        value = jnp.where(live, value, 0.0).astype(out_ref.dtype)
        for copy in range(out_ref.shape[0]):
            out_ref[copy, :, span] = value


def mask_psi(left_sizes, right_sizes, psi):
    return pl.pallas_call(
        mask_kernel,
        out_shape=jax.ShapeDtypeStruct((NZ,) + psi.shape, psi.dtype),
        in_specs=[SMEM_SPEC, SMEM_SPEC, VMEM_SPEC],
        out_specs=VMEM_SPEC,
        name="mask_psi",
    )(left_sizes, right_sizes, psi)


def plan_kernel(own_ref, other_ref, slots_ref, rows_ref, next_ref):
    shape = own_ref.shape
    count = own_ref.size
    slots = [
        (side, pair, block, s)
        for side in range(2)
        for pair in range(shape[0])
        for block in range(shape[2])
        for s in range(shape[1])
    ]

    def row_of(slot):
        return (own_ref, other_ref)[slot[0]][slot[1], slot[3], slot[2]]

    for place in range(slots_ref.shape[0]):
        slots_ref[place] = 2 * count
    for place in range(rows_ref.shape[0]):
        rows_ref[place] = 0
    for row in range(shape[2]):
        next_ref[row] = 0
    for slot in slots:
        row = row_of(slot)
        next_ref[row] = next_ref[row] + 1
    start = jnp.int32(0)
    for row in range(shape[2]):
        pairs = (next_ref[row] + 1) // 2
        next_ref[row] = 2 * start

        @pl.loop(0, pairs)
        def _(i):
            rows_ref[start + i] = row

        start = start + pairs
    for number, slot in enumerate(slots):
        row = row_of(slot)
        place = next_ref[row]
        slots_ref[place] = number
        next_ref[row] = place + 1


def plan(own, other):
    pairs = own.size + own.shape[2] // 2
    return pl.pallas_call(
        plan_kernel,
        out_shape=(
            jax.ShapeDtypeStruct((2 * pairs,), jnp.int32),
            jax.ShapeDtypeStruct((pairs,), jnp.int32),
        ),
        in_specs=[SMEM_SPEC, SMEM_SPEC],
        out_specs=(SMEM_SPEC, SMEM_SPEC),
        scratch_shapes=[pltpu.SMEM((own.shape[2],), jnp.int32)],
        compiler_params=pltpu.CompilerParams(vmem_limit_bytes=SMALL_LIMIT),
        name="plan",
    )(own, other)


NEAR, AWAY = (0, 1), (3, 2)


def two_copies(twos, right, buffer, sem):
    _, xh, core, xl, y = position()
    x = xh * NXL + xl
    cols = right[0].shape[1]
    copies, halves = [], []
    for index, (step, places) in enumerate(twos):
        copies.append([])
        for way, place in enumerate(places):
            unit_x = jnp.where(core == 0, x ^ step, x ^ place)
            unit_y = jnp.where(core == 0, y ^ place, y ^ step)
            column = pl.multiple_of((lax.rem(unit_x, NXL) * NY + unit_y) * cols, BLK)
            for side in range(2):
                copies[-1].append(
                    pltpu.make_async_copy(
                        right[side].at[:, :, pl.ds(column, cols)],
                        buffer.at[index, side, :, :, pl.ds(way * cols, cols)],
                        sem.at[index, side, way],
                    )
                )
        halves.append(unit_x // NXL)
    return copies, halves


def wide(array):
    rows = array.shape[1] * array.shape[2]
    return jnp.concatenate([array[way].reshape(rows, array.shape[3]) for way in range(2)], axis=1)


def times(left_side, right_side):
    return lax.dot_general(
        left_side, right_side, (((1,), (1,)), ((), ())), preferred_element_type=jnp.float32
    )


def operator(buffer, index, side):
    return buffer[index, side].reshape(buffer.shape[2] * buffer.shape[3], buffer.shape[4])


def sums_kernel(twos, ahead, *refs):
    refs = list(refs)
    acc_in = refs.pop(0) if ahead else None
    arrays = [refs.pop(0) for _ in twos]
    right = (refs.pop(0), refs.pop(0))
    left = None if ahead else (refs.pop(0), refs.pop(0))
    acc, later_ref, rbuf, sem, later_sem = refs
    copies, halves = two_copies(twos, right, rbuf, sem)
    if ahead:
        later = sum(two_copies(ahead, right, later_ref, later_sem)[0], [])
    else:
        count = left[0].shape[0]
        later = [
            pltpu.make_async_copy(
                left[side], later_ref.at[pl.ds(side * count, count)], later_sem.at[side]
            )
            for side in range(2)
        ]
        later_ref[2 * count] = jnp.zeros(later_ref.shape[1:], later_ref.dtype)
    for copy in sum(copies, []) + later:
        copy.start()
    acc[...] = acc_in[...] if ahead else jnp.zeros_like(acc)
    for index, array in enumerate(arrays):
        for copy in copies[index]:
            copy.wait()

        @pl.loop(0, 2)
        def _(side):
            acc[halves[index], side] += times(wide(array), operator(rbuf, index, side))

    for copy in later:
        copy.wait()


def sums(acc, pieces, right, left=None, ahead=()):
    arrays = [array for array, _, _ in pieces]
    twos = tuple((step, places) for _, step, places in pieces)
    group, cols = arrays[0].shape[2:]
    pairs = right[0].shape[0]
    units = 2 * len(arrays)
    near, away = ([acc] if ahead else []) + arrays, list(right) + ([] if ahead else list(left))
    if ahead:
        later = (2, 2, pairs, cols, 2 * cols)
    else:
        later = (2 * left[0].shape[0] + 1,) + left[0].shape[1:]
    return pl.pallas_call(
        functools.partial(sums_kernel, twos, ahead),
        out_shape=[
            jax.ShapeDtypeStruct((NXH, 2, NZ * group, pairs * cols), jnp.float32),
            jax.ShapeDtypeStruct(later, jnp.bfloat16),
        ],
        in_specs=[VMEM_SPEC] * len(near) + [HBM_SPEC] * len(away),
        out_specs=[VMEM_SPEC] * 2,
        scratch_shapes=[
            pltpu.VMEM((units // 2, 2, pairs, cols, 2 * cols), jnp.bfloat16),
            pltpu.SemaphoreType.DMA((units // 2, 2, 2)),
            pltpu.SemaphoreType.DMA((2, 2, 2) if ahead else (2,)),
        ],
        input_output_aliases={0: 0} if ahead else {},
        compiler_params=pltpu.CompilerParams(vmem_limit_bytes=VMEM_LIMIT),
        cost_estimate=pl.CostEstimate(
            flops=2 * units * 2 * pairs * NZ * group * cols * cols,
            bytes_accessed=units * 2 * pairs * cols * cols * 2,
            transcendentals=0,
        ),
        name=f"sums_{units}",
    )(*near, *away)


UNROLL = 6


def terms_kernel(slots_ref, rows_ref, sizes_ref, right_ref, acc, far_near, far_away, far_ref, left_ref, *refs):
    keep_ref, send_ref, part, total = refs
    z, xh, core, xl, y = position()
    arrays = (far_near, far_away)
    group, cols = far_near.shape[2:]
    pairs = far_ref.shape[2]
    lane = lax.broadcasted_iota(jnp.int32, (1, BLK), 1)
    start = (xl * NY + y) * (cols // BLK)
    live = jnp.concatenate(
        [(lane < right_ref[start + i]).astype(jnp.float32) for i in range(cols // BLK)], axis=1
    )
    height = total.shape[0]
    total[...] = jnp.zeros_like(total)
    for pair in range(2 * pairs):
        for q in range(NZ * NXH):
            at = pl.multiple_of(pair * height + (q * NC + 1 - core) * group, 16)
            part[pl.ds(at, group), :] = jnp.zeros((group, cols), part.dtype)

    def place(half, side, values):
        for pair in range(pairs):
            rounded = (values[:, pair * cols : (pair + 1) * cols] * live).astype(part.dtype)
            for dz in range(NZ):
                at = (side * pairs + pair) * height + ((dz * NXH + half) * NC + core) * group
                part[pl.ds(pl.multiple_of(at, 16), group), :] = rounded[dz * group : (dz + 1) * group]

    @pl.loop(0, 2)
    def _(side):
        @pl.when(core == 0)
        def _():
            far = 1 - xh
            place(xh, side, acc[xh, side])
            left_side = jnp.concatenate([wide(array) for array in arrays], axis=1)
            right_side = jnp.concatenate([operator(far_ref, i, side) for i in range(2)], axis=1)
            place(far, side, acc[far, side] + times(left_side, right_side))

        @pl.when(core == 1)
        def _():
            for index, (array, half) in enumerate(zip(arrays, (xh, 1 - xh))):
                place(half, side, acc[half, side] + times(wide(array), operator(far_ref, index, side)))

    last_block = 2 * pairs * height // BLK - 1

    @pl.loop(0, rows_ref.shape[0] // UNROLL)
    def _(step):
        for turn in range(UNROLL):
            number = step * UNROLL + turn
            slots = [slots_ref[2 * number + way] for way in range(2)]
            blocks = [jnp.minimum(slot // 2, last_block) for slot in slots]
            result = jnp.dot(
                jnp.concatenate([left_ref[slot] for slot in slots], axis=1),
                jnp.concatenate(
                    [part[pl.ds(pl.multiple_of(block * BLK, BLK), BLK), :] for block in blocks], axis=0
                ),
                preferred_element_type=jnp.float32,
            )
            total[pl.ds(pl.multiple_of(rows_ref[number] * BLK, BLK), BLK), :] += result

    for step in range(NZ * NXH):
        q = (z * NXH + xh) ^ step
        mine = pl.multiple_of((q * NC + core) * group, 16)
        theirs = pl.multiple_of((q * NC + 1 - core) * group, 16)
        keep_ref[step] = jnp.where(row_live(mine, sizes_ref, group), total[pl.ds(mine, group), :], 0.0)
        other = jnp.where(row_live(theirs, sizes_ref, group), total[pl.ds(theirs, group), :], 0.0)
        send_ref[step] = other.astype(send_ref.dtype)


def terms(slots, rows, left_sizes, right_sizes, acc, far_near, far_away, far, left):
    group, cols = far_near.shape[2:]
    height = NZ * NXH * NC * group
    pairs = 2 * far.shape[2]
    assert rows.shape[0] % UNROLL == 0
    return pl.pallas_call(
        terms_kernel,
        out_shape=(
            jax.ShapeDtypeStruct((NZ * NXH, group, cols), jnp.float32),
            jax.ShapeDtypeStruct((NZ * NXH, group, cols), jnp.bfloat16),
        ),
        in_specs=[SMEM_SPEC] * 4 + [VMEM_SPEC] * 5,
        out_specs=(VMEM_SPEC, VMEM_SPEC),
        scratch_shapes=[
            pltpu.VMEM((pairs * height, cols), jnp.bfloat16),
            pltpu.VMEM((height, cols), jnp.float32),
        ],
        compiler_params=pltpu.CompilerParams(vmem_limit_bytes=VMEM_LIMIT),
        name="terms",
    )(slots, rows, left_sizes, right_sizes, acc, far_near, far_away, far, left)


def local(psi, left_ops, a_rows, right_ops, left_sizes, right_sizes):
    copies = mask_psi(left_sizes, right_sizes, psi)
    right = (right_ops, core_swap(right_ops))
    flat_left = left_ops.reshape((-1, BLK, BLK))
    left = (flat_left, core_swap(flat_left))
    rows_by_slot = jnp.transpose(a_rows, (0, 2, 1))
    slots, rows = plan(rows_by_slot, core_swap(rows_by_slot))

    along_z = exchange(copies, z_groups())
    beside = partner(along_z, "middle", 1)
    across = partner(along_z, "middle", 3)
    beside, slots, rows = lax.optimization_barrier((beside, slots, rows))
    near = jnp.stack([along_z, beside])
    near_1 = partner(near, "last", 1)
    near_3 = partner(near, "last", 3)
    away = jnp.stack([across, partner(across, "middle", 1)])
    away_1 = partner(away, "last", 1)
    away_3 = partner(away, "last", 3)
    acc, both = sums(None, [(near, 0, NEAR), (away, 0, AWAY)], right, left)
    near_3, away_1, acc = lax.optimization_barrier((near_3, away_1, acc))
    near_2 = partner(near_3, "last", 1)
    away_2 = partner(away_1, "last", 3)
    acc, far = sums(
        acc,
        [(near_1, 1, NEAR), (near_3, 3, NEAR), (away_1, 1, AWAY), (away_3, 3, AWAY)],
        right,
        ahead=((2, NEAR), (2, AWAY)),
    )
    keep, send = terms(slots, rows, left_sizes, right_sizes, acc, near_2, away_2, far, both)
    chip = keep + core_swap(send).astype(jnp.float32)
    rounded = chip.astype(jnp.bfloat16)
    summed = chip[0]
    for step in range(1, NZ * NXH):
        summed = summed + to_owner(rounded[step], step).astype(jnp.float32)
    return summed


def solution(mesh):
    placed = (
        P("pair", "panel"),
        P("pair", None, None, None, None),
        P("pair", None, None),
        P("pair", "panel", None),
        P(),
        P(),
    )
    return jax.shard_map(
        local, mesh=mesh, in_specs=placed, out_specs=P("pair", "panel"), check_vma=False
    )
```

```python
import functools

import jax
import jax.numpy as jnp
from jax import lax
from jax.experimental import pallas as pl
from jax.experimental.pallas import tpu as pltpu
from jax.sharding import PartitionSpec as P

BLK = 128
NZ, NXH, NC, NXL, NY = 8, 2, 2, 2, 4
NX = NXH * NXL
AXES = ("pair", "panel")
VMEM_LIMIT = 28 * 1024 * 1024
SMALL_LIMIT = 2 * 1024 * 1024
SMEM_SPEC = pl.BlockSpec(memory_space=pltpu.SMEM)
VMEM_SPEC = pl.BlockSpec(memory_space=pltpu.VMEM)
HBM_SPEC = pl.BlockSpec(memory_space=pltpu.HBM)


def flat(z, x, y, core):
    pair = (z * NXH + x // NXL) * NC + core
    return pair * (NXL * NY) + (x % NXL) * NY + y


def everywhere():
    return [
        (z, x, y, core) for z in range(NZ) for x in range(NX) for y in range(NY) for core in range(NC)
    ]


def core_swap(value):
    return lax.ppermute(
        value, AXES, [(flat(z, x, y, 1 - c), flat(z, x, y, c)) for z, x, y, c in everywhere()]
    )


def partner(value, ring, step):
    perm = []
    for z, x, y, c in everywhere():
        along_x = (ring == "last") == (c == 0)
        source = flat(z, x ^ step, y, c) if along_x else flat(z, x, y ^ step, c)
        perm.append((source, flat(z, x, y, c)))
    return lax.ppermute(value, AXES, perm)


def exchange(copies, groups):
    return lax.all_to_all(
        copies, AXES, split_axis=0, concat_axis=0, axis_index_groups=groups, tiled=True
    )


def z_groups():
    return [
        [flat(z, x, y, c) for z in range(NZ)] for x in range(NX) for y in range(NY) for c in range(NC)
    ]


def position():
    pair, panel = lax.axis_index("pair"), lax.axis_index("panel")
    return pair // (NXH * NC), (pair // NC) % NXH, pair % NC, panel // NY, panel % NY


def row_live(base, left_ref, count):
    first = base // BLK
    second = jnp.minimum(first + 1, left_ref.shape[0] - 1)
    index = base + lax.broadcasted_iota(jnp.int32, (count, 1), 0)
    end = (first + 1) * BLK
    return index < jnp.where(index < end, first * BLK + left_ref[first], end + left_ref[second])


def mask_kernel(left_ref, right_ref, psi_ref, out_ref):
    rows, cols = psi_ref.shape
    panel = lax.axis_index("panel")
    rows_live = row_live(lax.axis_index("pair") * rows, left_ref, rows)
    lane = lax.broadcasted_iota(jnp.int32, (rows, BLK), 1)
    for block in range(cols // BLK):
        live = rows_live & (lane < right_ref[panel * (cols // BLK) + block])
        span = slice(block * BLK, (block + 1) * BLK)
        value = psi_ref[:, span].astype(jnp.float32)
        value = jnp.where(live, value, 0.0).astype(out_ref.dtype)
        for copy in range(out_ref.shape[0]):
            out_ref[copy, :, span] = value


def mask_psi(left_sizes, right_sizes, psi):
    return pl.pallas_call(
        mask_kernel,
        out_shape=jax.ShapeDtypeStruct((NZ,) + psi.shape, psi.dtype),
        in_specs=[SMEM_SPEC, SMEM_SPEC, VMEM_SPEC],
        out_specs=VMEM_SPEC,
        name="mask_psi",
    )(left_sizes, right_sizes, psi)


def plan_kernel(own_ref, other_ref, slots_ref, rows_ref, next_ref):
    shape = own_ref.shape
    count = own_ref.size
    slots = [
        (side, pair, block, s)
        for side in range(2)
        for pair in range(shape[0])
        for block in range(shape[2])
        for s in range(shape[1])
    ]

    def row_of(slot):
        return (own_ref, other_ref)[slot[0]][slot[1], slot[3], slot[2]]

    for place in range(slots_ref.shape[0]):
        slots_ref[place] = 2 * count
    for place in range(rows_ref.shape[0]):
        rows_ref[place] = 0
    for row in range(shape[2]):
        next_ref[row] = 0
    for slot in slots:
        row = row_of(slot)
        next_ref[row] = next_ref[row] + 1
    start = jnp.int32(0)
    for row in range(shape[2]):
        pairs = (next_ref[row] + 1) // 2
        next_ref[row] = 2 * start

        @pl.loop(0, pairs)
        def _(i):
            rows_ref[start + i] = row

        start = start + pairs
    for number, slot in enumerate(slots):
        row = row_of(slot)
        place = next_ref[row]
        slots_ref[place] = number
        next_ref[row] = place + 1


def plan(own, other):
    pairs = own.size + own.shape[2] // 2
    return pl.pallas_call(
        plan_kernel,
        out_shape=(
            jax.ShapeDtypeStruct((2 * pairs,), jnp.int32),
            jax.ShapeDtypeStruct((pairs,), jnp.int32),
        ),
        in_specs=[SMEM_SPEC, SMEM_SPEC],
        out_specs=(SMEM_SPEC, SMEM_SPEC),
        scratch_shapes=[pltpu.SMEM((own.shape[2],), jnp.int32)],
        compiler_params=pltpu.CompilerParams(vmem_limit_bytes=SMALL_LIMIT),
        name="plan",
    )(own, other)


NEAR, AWAY = (0, 1), (3, 2)


def two_copies(twos, right, buffer, sem):
    _, xh, core, xl, y = position()
    x = xh * NXL + xl
    cols = right[0].shape[1]
    copies, halves = [], []
    for index, (step, places) in enumerate(twos):
        copies.append([])
        for way, place in enumerate(places):
            unit_x = jnp.where(core == 0, x ^ step, x ^ place)
            unit_y = jnp.where(core == 0, y ^ place, y ^ step)
            column = pl.multiple_of((lax.rem(unit_x, NXL) * NY + unit_y) * cols, BLK)
            for side in range(2):
                copies[-1].append(
                    pltpu.make_async_copy(
                        right[side].at[:, :, pl.ds(column, cols)],
                        buffer.at[index, side, :, :, pl.ds(way * cols, cols)],
                        sem.at[index, side, way],
                    )
                )
        halves.append(unit_x // NXL)
    return copies, halves


def wide(array):
    rows = array.shape[1] * array.shape[2]
    return jnp.concatenate([array[way].reshape(rows, array.shape[3]) for way in range(2)], axis=1)


def times(left_side, right_side):
    return lax.dot_general(
        left_side, right_side, (((1,), (1,)), ((), ())), preferred_element_type=jnp.float32
    )


def operator(buffer, index, side):
    return buffer[index, side].reshape(buffer.shape[2] * buffer.shape[3], buffer.shape[4])


def sums_kernel(twos, first, ahead, *refs):
    refs = list(refs)
    acc_in = None if first else refs.pop(0)
    arrays = [refs.pop(0) for _ in twos]
    right = (refs.pop(0), refs.pop(0))
    left = (refs.pop(0), refs.pop(0)) if first else None
    acc = refs.pop(0)
    later_ref = refs.pop(0) if first or ahead else None
    rbuf, sem, later_sem = refs
    copies, halves = two_copies(twos, right, rbuf, sem)
    later = []
    if ahead:
        later = sum(two_copies(ahead, right, later_ref, later_sem)[0], [])
    if first:
        count = left[0].shape[0]
        later = [
            pltpu.make_async_copy(
                left[side], later_ref.at[pl.ds(side * count, count)], later_sem.at[side]
            )
            for side in range(2)
        ]
        later_ref[2 * count] = jnp.zeros(later_ref.shape[1:], later_ref.dtype)
    for copy in sum(copies, []) + later:
        copy.start()
    acc[...] = jnp.zeros_like(acc) if first else acc_in[...]
    for index, array in enumerate(arrays):
        for copy in copies[index]:
            copy.wait()

        @pl.loop(0, 2)
        def _(side):
            acc[halves[index], side] += times(wide(array), operator(rbuf, index, side))

    for copy in later:
        copy.wait()


def sums(acc, pieces, right, left=None, ahead=()):
    arrays = [array for array, _, _ in pieces]
    twos = tuple((step, places) for _, step, places in pieces)
    group, cols = arrays[0].shape[2:]
    pairs = right[0].shape[0]
    units = 2 * len(arrays)
    first = acc is None
    near, away = ([] if first else [acc]) + arrays, list(right) + (list(left) if first else [])
    out_shape = [jax.ShapeDtypeStruct((NXH, 2, NZ * group, pairs * cols), jnp.float32)]
    if first:
        later = (2 * left[0].shape[0] + 1,) + left[0].shape[1:]
        out_shape.append(jax.ShapeDtypeStruct(later, jnp.bfloat16))
    if ahead:
        out_shape.append(jax.ShapeDtypeStruct((2, 2, pairs, cols, 2 * cols), jnp.bfloat16))
    return pl.pallas_call(
        functools.partial(sums_kernel, twos, first, ahead),
        out_shape=out_shape,
        in_specs=[VMEM_SPEC] * len(near) + [HBM_SPEC] * len(away),
        out_specs=[VMEM_SPEC] * len(out_shape),
        scratch_shapes=[
            pltpu.VMEM((units // 2, 2, pairs, cols, 2 * cols), jnp.bfloat16),
            pltpu.SemaphoreType.DMA((units // 2, 2, 2)),
            pltpu.SemaphoreType.DMA((2, 2, 2) if ahead else (2,)),
        ],
        input_output_aliases={} if first else {0: 0},
        compiler_params=pltpu.CompilerParams(vmem_limit_bytes=VMEM_LIMIT),
        cost_estimate=pl.CostEstimate(
            flops=2 * units * 2 * pairs * NZ * group * cols * cols,
            bytes_accessed=units * 2 * pairs * cols * cols * 2,
            transcendentals=0,
        ),
        name=f"sums_{'first' if first else 'last' if ahead else 'middle'}",
    )(*near, *away)


UNROLL = 6


def terms_kernel(slots_ref, rows_ref, sizes_ref, right_ref, acc, far_near, far_away, far_ref, left_ref, *refs):
    keep_ref, send_ref, part, total = refs
    _, xh, core, xl, y = position()
    arrays = (far_near, far_away)
    group, cols = far_near.shape[2:]
    pairs = far_ref.shape[2]
    lane = lax.broadcasted_iota(jnp.int32, (1, BLK), 1)
    start = (xl * NY + y) * (cols // BLK)
    live = jnp.concatenate(
        [(lane < right_ref[start + i]).astype(jnp.float32) for i in range(cols // BLK)], axis=1
    )
    height = total.shape[0]
    total[...] = jnp.zeros_like(total)
    for pair in range(2 * pairs):
        for q in range(NZ * NXH):
            at = pl.multiple_of(pair * height + (q * NC + 1 - core) * group, 16)
            part[pl.ds(at, group), :] = jnp.zeros((group, cols), part.dtype)

    def place(half, side, values):
        for pair in range(pairs):
            rounded = (values[:, pair * cols : (pair + 1) * cols] * live).astype(part.dtype)
            for dz in range(NZ):
                at = (side * pairs + pair) * height + ((dz * NXH + half) * NC + core) * group
                part[pl.ds(pl.multiple_of(at, 16), group), :] = rounded[dz * group : (dz + 1) * group]

    @pl.loop(0, 2)
    def _(side):
        @pl.when(core == 0)
        def _():
            far = 1 - xh
            place(xh, side, acc[xh, side])
            left_side = jnp.concatenate([wide(array) for array in arrays], axis=1)
            right_side = jnp.concatenate([operator(far_ref, i, side) for i in range(2)], axis=1)
            place(far, side, acc[far, side] + times(left_side, right_side))

        @pl.when(core == 1)
        def _():
            for index, (array, half) in enumerate(zip(arrays, (xh, 1 - xh))):
                place(half, side, acc[half, side] + times(wide(array), operator(far_ref, index, side)))

    last_block = 2 * pairs * height // BLK - 1

    @pl.loop(0, rows_ref.shape[0] // UNROLL)
    def _(step):
        for turn in range(UNROLL):
            number = step * UNROLL + turn
            slots = [slots_ref[2 * number + way] for way in range(2)]
            blocks = [jnp.minimum(slot // 2, last_block) for slot in slots]
            result = jnp.dot(
                jnp.concatenate([left_ref[slot] for slot in slots], axis=1),
                jnp.concatenate(
                    [part[pl.ds(pl.multiple_of(block * BLK, BLK), BLK), :] for block in blocks], axis=0
                ),
                preferred_element_type=jnp.float32,
            )
            total[pl.ds(pl.multiple_of(rows_ref[number] * BLK, BLK), BLK), :] += result

    for q in range(NZ * NXH):
        mine = pl.multiple_of((q * NC + core) * group, 16)
        theirs = pl.multiple_of((q * NC + 1 - core) * group, 16)
        keep_ref[q] = jnp.where(row_live(mine, sizes_ref, group), total[pl.ds(mine, group), :], 0.0)
        other = jnp.where(row_live(theirs, sizes_ref, group), total[pl.ds(theirs, group), :], 0.0)
        send_ref[q] = other.astype(send_ref.dtype)


def terms(slots, rows, left_sizes, right_sizes, acc, far_near, far_away, far, left):
    group, cols = far_near.shape[2:]
    height = NZ * NXH * NC * group
    pairs = 2 * far.shape[2]
    assert rows.shape[0] % UNROLL == 0
    return pl.pallas_call(
        terms_kernel,
        out_shape=(
            jax.ShapeDtypeStruct((NZ * NXH, group, cols), jnp.float32),
            jax.ShapeDtypeStruct((NZ * NXH, group, cols), jnp.bfloat16),
        ),
        in_specs=[SMEM_SPEC] * 4 + [VMEM_SPEC] * 5,
        out_specs=(VMEM_SPEC, VMEM_SPEC),
        scratch_shapes=[
            pltpu.VMEM((pairs * height, cols), jnp.bfloat16),
            pltpu.VMEM((height, cols), jnp.float32),
        ],
        compiler_params=pltpu.CompilerParams(vmem_limit_bytes=VMEM_LIMIT),
        name="terms",
    )(slots, rows, left_sizes, right_sizes, acc, far_near, far_away, far, left)


def local(psi, left_ops, a_rows, right_ops, left_sizes, right_sizes):
    copies = mask_psi(left_sizes, right_sizes, psi)
    right = (right_ops, core_swap(right_ops))
    flat_left = left_ops.reshape((-1, BLK, BLK))
    left = (flat_left, core_swap(flat_left))
    rows_by_slot = jnp.transpose(a_rows, (0, 2, 1))
    rows_other = core_swap(rows_by_slot)

    along_z = exchange(copies, z_groups())
    beside = partner(along_z, "middle", 1)
    across = partner(along_z, "middle", 3)
    opposite = partner(across, "middle", 1)
    near, away = jnp.stack([along_z, beside]), jnp.stack([across, opposite])
    near_3 = partner(near, "last", 3)
    near, rows_other = lax.optimization_barrier((near, rows_other))
    slots, rows = plan(rows_by_slot, rows_other)
    near, away, slots, rows = lax.optimization_barrier((near, away, slots, rows))
    away_1 = partner(away, "last", 1)
    near_1 = partner(near, "last", 1)
    away_3 = partner(away, "last", 3)
    acc, both = sums(None, [(near, 0, NEAR), (away, 0, AWAY)], right, left)
    near_3, away_1, acc = lax.optimization_barrier((near_3, away_1, acc))
    near_2 = partner(near_3, "last", 1)
    away_2 = partner(away_1, "last", 3)
    (acc,) = sums(acc, [(near_3, 3, NEAR), (away_1, 1, AWAY)], right)
    acc, far = sums(
        acc, [(near_1, 1, NEAR), (away_3, 3, AWAY)], right, ahead=((2, NEAR), (2, AWAY))
    )
    keep, send = terms(slots, rows, left_sizes, right_sizes, acc, near_2, away_2, far, both)
    mine = (keep + core_swap(send).astype(jnp.float32)).astype(jnp.bfloat16)
    groups = [
        [flat(z, xh * NXL + xl, y, c) for z in range(NZ) for xh in range(NXH)]
        for c in range(NC)
        for xl in range(NXL)
        for y in range(NY)
    ]
    parts = exchange(mine, groups)
    return parts.astype(jnp.float32).sum(axis=0)


def solution(mesh):
    placed = (
        P("pair", "panel"),
        P("pair", None, None, None, None),
        P("pair", None, None),
        P("pair", "panel", None),
        P(),
        P(),
    )
    return jax.shard_map(
        local, mesh=mesh, in_specs=placed, out_specs=P("pair", "panel"), check_vma=False
    )
```

```python
import functools

import jax
import jax.numpy as jnp
from jax import lax
from jax.experimental import pallas as pl
from jax.experimental.pallas import tpu as pltpu
from jax.sharding import PartitionSpec as P

BLK = 128
NZ, NXH, NC, NXL, NY = 8, 2, 2, 2, 4
NX = NXH * NXL
AXES = ("pair", "panel")
VMEM_LIMIT = 28 * 1024 * 1024
SMALL_LIMIT = 2 * 1024 * 1024
SMEM_SPEC = pl.BlockSpec(memory_space=pltpu.SMEM)
VMEM_SPEC = pl.BlockSpec(memory_space=pltpu.VMEM)
HBM_SPEC = pl.BlockSpec(memory_space=pltpu.HBM)


def flat(z, x, y, core):
    pair = (z * NXH + x // NXL) * NC + core
    return pair * (NXL * NY) + (x % NXL) * NY + y


def everywhere():
    return [
        (z, x, y, core) for z in range(NZ) for x in range(NX) for y in range(NY) for core in range(NC)
    ]


def core_swap(value):
    return lax.ppermute(
        value, AXES, [(flat(z, x, y, 1 - c), flat(z, x, y, c)) for z, x, y, c in everywhere()]
    )


def partner(value, ring, step):
    perm = []
    for z, x, y, c in everywhere():
        along_x = (ring == "last") == (c == 0)
        source = flat(z, x ^ step, y, c) if along_x else flat(z, x, y ^ step, c)
        perm.append((source, flat(z, x, y, c)))
    return lax.ppermute(value, AXES, perm)


def exchange(copies, groups):
    return lax.all_to_all(
        copies, AXES, split_axis=0, concat_axis=0, axis_index_groups=groups, tiled=True
    )


def z_groups():
    return [
        [flat(z, x, y, c) for z in range(NZ)] for x in range(NX) for y in range(NY) for c in range(NC)
    ]


def position():
    pair, panel = lax.axis_index("pair"), lax.axis_index("panel")
    return pair // (NXH * NC), (pair // NC) % NXH, pair % NC, panel // NY, panel % NY


def row_live(base, left_ref, count):
    first = base // BLK
    second = jnp.minimum(first + 1, left_ref.shape[0] - 1)
    index = base + lax.broadcasted_iota(jnp.int32, (count, 1), 0)
    end = (first + 1) * BLK
    return index < jnp.where(index < end, first * BLK + left_ref[first], end + left_ref[second])


def mask_kernel(left_ref, right_ref, psi_ref, out_ref):
    rows, cols = psi_ref.shape
    panel = lax.axis_index("panel")
    rows_live = row_live(lax.axis_index("pair") * rows, left_ref, rows)
    lane = lax.broadcasted_iota(jnp.int32, (rows, BLK), 1)
    for block in range(cols // BLK):
        live = rows_live & (lane < right_ref[panel * (cols // BLK) + block])
        span = slice(block * BLK, (block + 1) * BLK)
        value = psi_ref[:, span].astype(jnp.float32)
        value = jnp.where(live, value, 0.0).astype(out_ref.dtype)
        for copy in range(out_ref.shape[0]):
            out_ref[copy, :, span] = value


def mask_psi(left_sizes, right_sizes, psi):
    return pl.pallas_call(
        mask_kernel,
        out_shape=jax.ShapeDtypeStruct((NZ,) + psi.shape, psi.dtype),
        in_specs=[SMEM_SPEC, SMEM_SPEC, VMEM_SPEC],
        out_specs=VMEM_SPEC,
        name="mask_psi",
    )(left_sizes, right_sizes, psi)


def plan_kernel(own_ref, other_ref, slots_ref, rows_ref, next_ref):
    shape = own_ref.shape
    count = own_ref.size
    slots = [
        (side, pair, block, s)
        for side in range(2)
        for pair in range(shape[0])
        for block in range(shape[2])
        for s in range(shape[1])
    ]

    def row_of(slot):
        return (own_ref, other_ref)[slot[0]][slot[1], slot[3], slot[2]]

    for place in range(slots_ref.shape[0]):
        slots_ref[place] = 2 * count
    for place in range(rows_ref.shape[0]):
        rows_ref[place] = 0
    for row in range(shape[2]):
        next_ref[row] = 0
    for slot in slots:
        row = row_of(slot)
        next_ref[row] = next_ref[row] + 1
    start = jnp.int32(0)
    for row in range(shape[2]):
        pairs = (next_ref[row] + 1) // 2
        next_ref[row] = 2 * start

        @pl.loop(0, pairs)
        def _(i):
            rows_ref[start + i] = row

        start = start + pairs
    for number, slot in enumerate(slots):
        row = row_of(slot)
        place = next_ref[row]
        slots_ref[place] = number
        next_ref[row] = place + 1


def plan(own, other):
    pairs = own.size + own.shape[2] // 2
    return pl.pallas_call(
        plan_kernel,
        out_shape=(
            jax.ShapeDtypeStruct((2 * pairs,), jnp.int32),
            jax.ShapeDtypeStruct((pairs,), jnp.int32),
        ),
        in_specs=[SMEM_SPEC, SMEM_SPEC],
        out_specs=(SMEM_SPEC, SMEM_SPEC),
        scratch_shapes=[pltpu.SMEM((own.shape[2],), jnp.int32)],
        compiler_params=pltpu.CompilerParams(vmem_limit_bytes=SMALL_LIMIT),
        name="plan",
    )(own, other)


NEAR, AWAY = (0, 1), (3, 2)


def two_copies(twos, right, buffer, sem):
    _, xh, core, xl, y = position()
    x = xh * NXL + xl
    cols = right[0].shape[1]
    copies, halves = [], []
    for index, (step, places) in enumerate(twos):
        copies.append([])
        for way, place in enumerate(places):
            unit_x = jnp.where(core == 0, x ^ step, x ^ place)
            unit_y = jnp.where(core == 0, y ^ place, y ^ step)
            column = pl.multiple_of((lax.rem(unit_x, NXL) * NY + unit_y) * cols, BLK)
            for side in range(2):
                copies[-1].append(
                    pltpu.make_async_copy(
                        right[side].at[:, :, pl.ds(column, cols)],
                        buffer.at[index, side, :, :, pl.ds(way * cols, cols)],
                        sem.at[index, side, way],
                    )
                )
        halves.append(unit_x // NXL)
    return copies, halves


def wide(array):
    rows = array.shape[1] * array.shape[2]
    return jnp.concatenate([array[way].reshape(rows, array.shape[3]) for way in range(2)], axis=1)


def times(left_side, right_side):
    return lax.dot_general(
        left_side, right_side, (((1,), (1,)), ((), ())), preferred_element_type=jnp.float32
    )


def operator(buffer, index, side):
    return buffer[index, side].reshape(buffer.shape[2] * buffer.shape[3], buffer.shape[4])


def sums_kernel(twos, first, ahead, *refs):
    refs = list(refs)
    acc_in = None if first else refs.pop(0)
    arrays = [refs.pop(0) for _ in twos]
    right = (refs.pop(0), refs.pop(0))
    left = (refs.pop(0), refs.pop(0)) if first else None
    acc = refs.pop(0)
    later_ref = refs.pop(0) if first or ahead else None
    rbuf, sem, later_sem = refs
    copies, halves = two_copies(twos, right, rbuf, sem)
    later = []
    if ahead:
        later = sum(two_copies(ahead, right, later_ref, later_sem)[0], [])
    if first:
        count = left[0].shape[0]
        later = [
            pltpu.make_async_copy(
                left[side], later_ref.at[pl.ds(side * count, count)], later_sem.at[side]
            )
            for side in range(2)
        ]
        later_ref[2 * count] = jnp.zeros(later_ref.shape[1:], later_ref.dtype)
    for copy in sum(copies, []) + later:
        copy.start()
    acc[...] = jnp.zeros_like(acc) if first else acc_in[...]
    for index, array in enumerate(arrays):
        for copy in copies[index]:
            copy.wait()

        @pl.loop(0, 2)
        def _(side):
            acc[halves[index], side] += times(wide(array), operator(rbuf, index, side))

    for copy in later:
        copy.wait()


def sums(acc, pieces, right, left=None, ahead=()):
    arrays = [array for array, _, _ in pieces]
    twos = tuple((step, places) for _, step, places in pieces)
    group, cols = arrays[0].shape[2:]
    pairs = right[0].shape[0]
    units = 2 * len(arrays)
    first = acc is None
    near, away = ([] if first else [acc]) + arrays, list(right) + (list(left) if first else [])
    out_shape = [jax.ShapeDtypeStruct((NXH, 2, NZ * group, pairs * cols), jnp.float32)]
    if first:
        later = (2 * left[0].shape[0] + 1,) + left[0].shape[1:]
        out_shape.append(jax.ShapeDtypeStruct(later, jnp.bfloat16))
    if ahead:
        out_shape.append(jax.ShapeDtypeStruct((2, 2, pairs, cols, 2 * cols), jnp.bfloat16))
    return pl.pallas_call(
        functools.partial(sums_kernel, twos, first, ahead),
        out_shape=out_shape,
        in_specs=[VMEM_SPEC] * len(near) + [HBM_SPEC] * len(away),
        out_specs=[VMEM_SPEC] * len(out_shape),
        scratch_shapes=[
            pltpu.VMEM((units // 2, 2, pairs, cols, 2 * cols), jnp.bfloat16),
            pltpu.SemaphoreType.DMA((units // 2, 2, 2)),
            pltpu.SemaphoreType.DMA((2, 2, 2) if ahead else (2,)),
        ],
        input_output_aliases={} if first else {0: 0},
        compiler_params=pltpu.CompilerParams(vmem_limit_bytes=VMEM_LIMIT),
        cost_estimate=pl.CostEstimate(
            flops=2 * units * 2 * pairs * NZ * group * cols * cols,
            bytes_accessed=units * 2 * pairs * cols * cols * 2,
            transcendentals=0,
        ),
        name=f"sums_{'first' if first else 'last' if ahead else 'middle'}",
    )(*near, *away)


UNROLL = 6


def terms_kernel(slots_ref, rows_ref, sizes_ref, right_ref, acc, far_near, far_away, far_ref, left_ref, *refs):
    keep_ref, send_ref, part, total = refs
    _, xh, core, xl, y = position()
    arrays = (far_near, far_away)
    group, cols = far_near.shape[2:]
    pairs = far_ref.shape[2]
    lane = lax.broadcasted_iota(jnp.int32, (1, BLK), 1)
    start = (xl * NY + y) * (cols // BLK)
    live = jnp.concatenate(
        [(lane < right_ref[start + i]).astype(jnp.float32) for i in range(cols // BLK)], axis=1
    )
    height = total.shape[0]
    total[...] = jnp.zeros_like(total)
    for pair in range(2 * pairs):
        for q in range(NZ * NXH):
            at = pl.multiple_of(pair * height + (q * NC + 1 - core) * group, 16)
            part[pl.ds(at, group), :] = jnp.zeros((group, cols), part.dtype)

    def place(half, side, values):
        for pair in range(pairs):
            rounded = (values[:, pair * cols : (pair + 1) * cols] * live).astype(part.dtype)
            for dz in range(NZ):
                at = (side * pairs + pair) * height + ((dz * NXH + half) * NC + core) * group
                part[pl.ds(pl.multiple_of(at, 16), group), :] = rounded[dz * group : (dz + 1) * group]

    @pl.loop(0, 2)
    def _(side):
        @pl.when(core == 0)
        def _():
            far = 1 - xh
            place(xh, side, acc[xh, side])
            left_side = jnp.concatenate([wide(array) for array in arrays], axis=1)
            right_side = jnp.concatenate([operator(far_ref, i, side) for i in range(2)], axis=1)
            place(far, side, acc[far, side] + times(left_side, right_side))

        @pl.when(core == 1)
        def _():
            for index, (array, half) in enumerate(zip(arrays, (xh, 1 - xh))):
                place(half, side, acc[half, side] + times(wide(array), operator(far_ref, index, side)))

    last_block = 2 * pairs * height // BLK - 1

    @pl.loop(0, rows_ref.shape[0] // UNROLL)
    def _(step):
        for turn in range(UNROLL):
            number = step * UNROLL + turn
            slots = [slots_ref[2 * number + way] for way in range(2)]
            blocks = [jnp.minimum(slot // 2, last_block) for slot in slots]
            result = jnp.dot(
                jnp.concatenate([left_ref[slot] for slot in slots], axis=1),
                jnp.concatenate(
                    [part[pl.ds(pl.multiple_of(block * BLK, BLK), BLK), :] for block in blocks], axis=0
                ),
                preferred_element_type=jnp.float32,
            )
            total[pl.ds(pl.multiple_of(rows_ref[number] * BLK, BLK), BLK), :] += result

    for q in range(NZ * NXH):
        mine = pl.multiple_of((q * NC + core) * group, 16)
        theirs = pl.multiple_of((q * NC + 1 - core) * group, 16)
        keep_ref[q] = jnp.where(row_live(mine, sizes_ref, group), total[pl.ds(mine, group), :], 0.0)
        other = jnp.where(row_live(theirs, sizes_ref, group), total[pl.ds(theirs, group), :], 0.0)
        send_ref[q] = other.astype(send_ref.dtype)


def terms(slots, rows, left_sizes, right_sizes, acc, far_near, far_away, far, left):
    group, cols = far_near.shape[2:]
    height = NZ * NXH * NC * group
    pairs = 2 * far.shape[2]
    assert rows.shape[0] % UNROLL == 0
    return pl.pallas_call(
        terms_kernel,
        out_shape=(
            jax.ShapeDtypeStruct((NZ * NXH, group, cols), jnp.float32),
            jax.ShapeDtypeStruct((NZ * NXH, group, cols), jnp.bfloat16),
        ),
        in_specs=[SMEM_SPEC] * 4 + [VMEM_SPEC] * 5,
        out_specs=(VMEM_SPEC, VMEM_SPEC),
        scratch_shapes=[
            pltpu.VMEM((pairs * height, cols), jnp.bfloat16),
            pltpu.VMEM((height, cols), jnp.float32),
        ],
        compiler_params=pltpu.CompilerParams(vmem_limit_bytes=VMEM_LIMIT),
        name="terms",
    )(slots, rows, left_sizes, right_sizes, acc, far_near, far_away, far, left)


def local(psi, left_ops, a_rows, right_ops, left_sizes, right_sizes):
    copies = mask_psi(left_sizes, right_sizes, psi)
    right = (right_ops, core_swap(right_ops))
    flat_left = left_ops.reshape((-1, BLK, BLK))
    left = (flat_left, core_swap(flat_left))
    rows_by_slot = jnp.transpose(a_rows, (0, 2, 1))
    rows_other = core_swap(rows_by_slot)

    along_z = exchange(copies, z_groups())
    beside = partner(along_z, "middle", 1)
    across = partner(along_z, "middle", 3)
    opposite = partner(across, "middle", 1)
    near, away = jnp.stack([along_z, beside]), jnp.stack([across, opposite])
    near_3 = partner(near, "last", 3)
    near, away, rows_other, right, left = lax.optimization_barrier((near, away, rows_other, right, left))
    away_1 = partner(away, "last", 1)
    near_1 = partner(near, "last", 1)
    away_3 = partner(away, "last", 3)
    slots, rows = plan(rows_by_slot, rows_other)
    near, slots, rows = lax.optimization_barrier((near, slots, rows))
    acc, both = sums(None, [(near, 0, NEAR), (away, 0, AWAY)], right, left)
    near_3, away_1, acc = lax.optimization_barrier((near_3, away_1, acc))
    near_2 = partner(near_3, "last", 1)
    away_2 = partner(away_1, "last", 3)
    (acc,) = sums(acc, [(near_3, 3, NEAR), (away_1, 1, AWAY)], right)
    acc, far = sums(
        acc, [(near_1, 1, NEAR), (away_3, 3, AWAY)], right, ahead=((2, NEAR), (2, AWAY))
    )
    keep, send = terms(slots, rows, left_sizes, right_sizes, acc, near_2, away_2, far, both)
    mine = (keep + core_swap(send).astype(jnp.float32)).astype(jnp.bfloat16)
    groups = [
        [flat(z, xh * NXL + xl, y, c) for z in range(NZ) for xh in range(NXH)]
        for c in range(NC)
        for xl in range(NXL)
        for y in range(NY)
    ]
    parts = exchange(mine, groups)
    return parts.astype(jnp.float32).sum(axis=0)


def solution(mesh):
    placed = (
        P("pair", "panel"),
        P("pair", None, None, None, None),
        P("pair", None, None),
        P("pair", "panel", None),
        P(),
        P(),
    )
    return jax.shard_map(
        local, mesh=mesh, in_specs=placed, out_specs=P("pair", "panel"), check_vma=False
    )
```

```python
import functools

import jax
import jax.numpy as jnp
from jax import lax
from jax.experimental import pallas as pl
from jax.experimental.pallas import tpu as pltpu
from jax.sharding import PartitionSpec as P

BLK = 128
NZ, NXH, NC, NXL, NY = 8, 2, 2, 2, 4
NX = NXH * NXL
AXES = ("pair", "panel")
VMEM_LIMIT = 28 * 1024 * 1024
SMALL_LIMIT = 2 * 1024 * 1024
SMEM_SPEC = pl.BlockSpec(memory_space=pltpu.SMEM)
VMEM_SPEC = pl.BlockSpec(memory_space=pltpu.VMEM)
HBM_SPEC = pl.BlockSpec(memory_space=pltpu.HBM)


def flat(z, x, y, core):
    pair = (z * NXH + x // NXL) * NC + core
    return pair * (NXL * NY) + (x % NXL) * NY + y


def everywhere():
    return [
        (z, x, y, core) for z in range(NZ) for x in range(NX) for y in range(NY) for core in range(NC)
    ]


def core_swap(value):
    return lax.ppermute(
        value, AXES, [(flat(z, x, y, 1 - c), flat(z, x, y, c)) for z, x, y, c in everywhere()]
    )


def partner(value, ring, step):
    perm = []
    for z, x, y, c in everywhere():
        along_x = (ring == "last") == (c == 0)
        source = flat(z, x ^ step, y, c) if along_x else flat(z, x, y ^ step, c)
        perm.append((source, flat(z, x, y, c)))
    return lax.ppermute(value, AXES, perm)


def exchange(copies, groups):
    return lax.all_to_all(
        copies, AXES, split_axis=0, concat_axis=0, axis_index_groups=groups, tiled=True
    )


def z_groups():
    return [
        [flat(z, x, y, c) for z in range(NZ)] for x in range(NX) for y in range(NY) for c in range(NC)
    ]


def position():
    pair, panel = lax.axis_index("pair"), lax.axis_index("panel")
    return pair // (NXH * NC), (pair // NC) % NXH, pair % NC, panel // NY, panel % NY


def row_live(base, left_ref, count):
    first = base // BLK
    second = jnp.minimum(first + 1, left_ref.shape[0] - 1)
    index = base + lax.broadcasted_iota(jnp.int32, (count, 1), 0)
    end = (first + 1) * BLK
    return index < jnp.where(index < end, first * BLK + left_ref[first], end + left_ref[second])


def mask_kernel(left_ref, right_ref, psi_ref, out_ref):
    rows, cols = psi_ref.shape
    panel = lax.axis_index("panel")
    rows_live = row_live(lax.axis_index("pair") * rows, left_ref, rows)
    lane = lax.broadcasted_iota(jnp.int32, (rows, BLK), 1)
    for block in range(cols // BLK):
        live = rows_live & (lane < right_ref[panel * (cols // BLK) + block])
        span = slice(block * BLK, (block + 1) * BLK)
        value = psi_ref[:, span].astype(jnp.float32)
        value = jnp.where(live, value, 0.0).astype(out_ref.dtype)
        for copy in range(out_ref.shape[0]):
            out_ref[copy, :, span] = value


def mask_psi(left_sizes, right_sizes, psi):
    return pl.pallas_call(
        mask_kernel,
        out_shape=jax.ShapeDtypeStruct((NZ,) + psi.shape, psi.dtype),
        in_specs=[SMEM_SPEC, SMEM_SPEC, VMEM_SPEC],
        out_specs=VMEM_SPEC,
        name="mask_psi",
    )(left_sizes, right_sizes, psi)


def plan_kernel(own_ref, other_ref, slots_ref, rows_ref, next_ref):
    shape = own_ref.shape
    count = own_ref.size
    slots = [
        (side, pair, block, s)
        for side in range(2)
        for pair in range(shape[0])
        for block in range(shape[2])
        for s in range(shape[1])
    ]

    def row_of(slot):
        return (own_ref, other_ref)[slot[0]][slot[1], slot[3], slot[2]]

    for place in range(slots_ref.shape[0]):
        slots_ref[place] = 2 * count
    for place in range(rows_ref.shape[0]):
        rows_ref[place] = 0
    for row in range(shape[2]):
        next_ref[row] = 0
    for slot in slots:
        row = row_of(slot)
        next_ref[row] = next_ref[row] + 1
    start = jnp.int32(0)
    for row in range(shape[2]):
        pairs = (next_ref[row] + 1) // 2
        next_ref[row] = 2 * start

        @pl.loop(0, pairs)
        def _(i):
            rows_ref[start + i] = row

        start = start + pairs
    for number, slot in enumerate(slots):
        row = row_of(slot)
        place = next_ref[row]
        slots_ref[place] = number
        next_ref[row] = place + 1


def plan(own, other):
    pairs = own.size + own.shape[2] // 2
    return pl.pallas_call(
        plan_kernel,
        out_shape=(
            jax.ShapeDtypeStruct((2 * pairs,), jnp.int32),
            jax.ShapeDtypeStruct((pairs,), jnp.int32),
        ),
        in_specs=[SMEM_SPEC, SMEM_SPEC],
        out_specs=(SMEM_SPEC, SMEM_SPEC),
        scratch_shapes=[pltpu.SMEM((own.shape[2],), jnp.int32)],
        compiler_params=pltpu.CompilerParams(vmem_limit_bytes=SMALL_LIMIT),
        name="plan",
    )(own, other)


NEAR, AWAY = (0, 1), (3, 2)


def two_copies(twos, right, buffer, sem):
    _, xh, core, xl, y = position()
    x = xh * NXL + xl
    cols = right[0].shape[1]
    copies, halves = [], []
    for index, (step, places) in enumerate(twos):
        copies.append([])
        for way, place in enumerate(places):
            unit_x = jnp.where(core == 0, x ^ step, x ^ place)
            unit_y = jnp.where(core == 0, y ^ place, y ^ step)
            column = pl.multiple_of((lax.rem(unit_x, NXL) * NY + unit_y) * cols, BLK)
            for side in range(2):
                copies[-1].append(
                    pltpu.make_async_copy(
                        right[side].at[:, :, pl.ds(column, cols)],
                        buffer.at[index, side, :, :, pl.ds(way * cols, cols)],
                        sem.at[index, side, way],
                    )
                )
        halves.append(unit_x // NXL)
    return copies, halves


def wide(array):
    rows = array.shape[1] * array.shape[2]
    return jnp.concatenate([array[way].reshape(rows, array.shape[3]) for way in range(2)], axis=1)


def times(left_side, right_side):
    return lax.dot_general(
        left_side, right_side, (((1,), (1,)), ((), ())), preferred_element_type=jnp.float32
    )


def operator(buffer, index, side):
    return buffer[index, side].reshape(buffer.shape[2] * buffer.shape[3], buffer.shape[4])


def sums_kernel(twos, first, ahead, *refs):
    refs = list(refs)
    acc_in = None if first else refs.pop(0)
    arrays = [refs.pop(0) for _ in twos]
    right = (refs.pop(0), refs.pop(0))
    left = (refs.pop(0), refs.pop(0)) if first else None
    acc = refs.pop(0)
    later_ref = refs.pop(0) if first or ahead else None
    rbuf, sem, later_sem = refs
    copies, halves = two_copies(twos, right, rbuf, sem)
    later = []
    if ahead:
        later = sum(two_copies(ahead, right, later_ref, later_sem)[0], [])
    if first:
        count = left[0].shape[0]
        later = [
            pltpu.make_async_copy(
                left[side], later_ref.at[pl.ds(side * count, count)], later_sem.at[side]
            )
            for side in range(2)
        ]
        later_ref[2 * count] = jnp.zeros(later_ref.shape[1:], later_ref.dtype)
    for copy in sum(copies, []) + later:
        copy.start()
    acc[...] = jnp.zeros_like(acc) if first else acc_in[...]
    for index, array in enumerate(arrays):
        for copy in copies[index]:
            copy.wait()

        @pl.loop(0, 2)
        def _(side):
            acc[halves[index], side] += times(wide(array), operator(rbuf, index, side))

    for copy in later:
        copy.wait()


def sums(acc, pieces, right, left=None, ahead=()):
    arrays = [array for array, _, _ in pieces]
    twos = tuple((step, places) for _, step, places in pieces)
    group, cols = arrays[0].shape[2:]
    pairs = right[0].shape[0]
    units = 2 * len(arrays)
    first = acc is None
    near, away = ([] if first else [acc]) + arrays, list(right) + (list(left) if first else [])
    out_shape = [jax.ShapeDtypeStruct((NXH, 2, NZ * group, pairs * cols), jnp.float32)]
    if first:
        later = (2 * left[0].shape[0] + 1,) + left[0].shape[1:]
        out_shape.append(jax.ShapeDtypeStruct(later, jnp.bfloat16))
    if ahead:
        out_shape.append(jax.ShapeDtypeStruct((2, 2, pairs, cols, 2 * cols), jnp.bfloat16))
    return pl.pallas_call(
        functools.partial(sums_kernel, twos, first, ahead),
        out_shape=out_shape,
        in_specs=[VMEM_SPEC] * len(near) + [HBM_SPEC] * len(away),
        out_specs=[VMEM_SPEC] * len(out_shape),
        scratch_shapes=[
            pltpu.VMEM((units // 2, 2, pairs, cols, 2 * cols), jnp.bfloat16),
            pltpu.SemaphoreType.DMA((units // 2, 2, 2)),
            pltpu.SemaphoreType.DMA((2, 2, 2) if ahead else (2,)),
        ],
        input_output_aliases={} if first else {0: 0},
        compiler_params=pltpu.CompilerParams(vmem_limit_bytes=VMEM_LIMIT),
        cost_estimate=pl.CostEstimate(
            flops=2 * units * 2 * pairs * NZ * group * cols * cols,
            bytes_accessed=units * 2 * pairs * cols * cols * 2,
            transcendentals=0,
        ),
        name=f"sums_{'first' if first else 'last' if ahead else 'middle'}",
    )(*near, *away)


UNROLL = 18


def terms_kernel(slots_ref, rows_ref, sizes_ref, right_ref, acc, far_near, far_away, far_ref, left_ref, *refs):
    keep_ref, send_ref, part, total = refs
    _, xh, core, xl, y = position()
    arrays = (far_near, far_away)
    group, cols = far_near.shape[2:]
    pairs = far_ref.shape[2]
    lane = lax.broadcasted_iota(jnp.int32, (1, BLK), 1)
    start = (xl * NY + y) * (cols // BLK)
    live = jnp.concatenate(
        [(lane < right_ref[start + i]).astype(jnp.float32) for i in range(cols // BLK)], axis=1
    )
    height = total.shape[0]
    total[...] = jnp.zeros_like(total)
    for pair in range(2 * pairs):
        for q in range(NZ * NXH):
            at = pl.multiple_of(pair * height + (q * NC + 1 - core) * group, 16)
            part[pl.ds(at, group), :] = jnp.zeros((group, cols), part.dtype)

    def place(half, side, values):
        for pair in range(pairs):
            rounded = (values[:, pair * cols : (pair + 1) * cols] * live).astype(part.dtype)
            for dz in range(NZ):
                at = (side * pairs + pair) * height + ((dz * NXH + half) * NC + core) * group
                part[pl.ds(pl.multiple_of(at, 16), group), :] = rounded[dz * group : (dz + 1) * group]

    @pl.loop(0, 2)
    def _(side):
        @pl.when(core == 0)
        def _():
            far = 1 - xh
            place(xh, side, acc[xh, side])
            left_side = jnp.concatenate([wide(array) for array in arrays], axis=1)
            right_side = jnp.concatenate([operator(far_ref, i, side) for i in range(2)], axis=1)
            place(far, side, acc[far, side] + times(left_side, right_side))

        @pl.when(core == 1)
        def _():
            for index, (array, half) in enumerate(zip(arrays, (xh, 1 - xh))):
                place(half, side, acc[half, side] + times(wide(array), operator(far_ref, index, side)))

    last_block = 2 * pairs * height // BLK - 1

    @pl.loop(0, rows_ref.shape[0] // UNROLL)
    def _(step):
        for turn in range(UNROLL):
            number = step * UNROLL + turn
            slots = [slots_ref[2 * number + way] for way in range(2)]
            blocks = [jnp.minimum(slot // 2, last_block) for slot in slots]
            result = jnp.dot(
                jnp.concatenate([left_ref[slot] for slot in slots], axis=1),
                jnp.concatenate(
                    [part[pl.ds(pl.multiple_of(block * BLK, BLK), BLK), :] for block in blocks], axis=0
                ),
                preferred_element_type=jnp.float32,
            )
            total[pl.ds(pl.multiple_of(rows_ref[number] * BLK, BLK), BLK), :] += result

    for q in range(NZ * NXH):
        mine = pl.multiple_of((q * NC + core) * group, 16)
        theirs = pl.multiple_of((q * NC + 1 - core) * group, 16)
        keep_ref[q] = jnp.where(row_live(mine, sizes_ref, group), total[pl.ds(mine, group), :], 0.0)
        other = jnp.where(row_live(theirs, sizes_ref, group), total[pl.ds(theirs, group), :], 0.0)
        send_ref[q] = other.astype(send_ref.dtype)


def terms(slots, rows, left_sizes, right_sizes, acc, far_near, far_away, far, left):
    group, cols = far_near.shape[2:]
    height = NZ * NXH * NC * group
    pairs = 2 * far.shape[2]
    assert rows.shape[0] % UNROLL == 0
    return pl.pallas_call(
        terms_kernel,
        out_shape=(
            jax.ShapeDtypeStruct((NZ * NXH, group, cols), jnp.float32),
            jax.ShapeDtypeStruct((NZ * NXH, group, cols), jnp.bfloat16),
        ),
        in_specs=[SMEM_SPEC] * 4 + [VMEM_SPEC] * 5,
        out_specs=(VMEM_SPEC, VMEM_SPEC),
        scratch_shapes=[
            pltpu.VMEM((pairs * height, cols), jnp.bfloat16),
            pltpu.VMEM((height, cols), jnp.float32),
        ],
        compiler_params=pltpu.CompilerParams(vmem_limit_bytes=VMEM_LIMIT),
        name="terms",
    )(slots, rows, left_sizes, right_sizes, acc, far_near, far_away, far, left)


def local(psi, left_ops, a_rows, right_ops, left_sizes, right_sizes):
    copies = mask_psi(left_sizes, right_sizes, psi)
    right = (right_ops, core_swap(right_ops))
    flat_left = left_ops.reshape((-1, BLK, BLK))
    left = (flat_left, core_swap(flat_left))
    rows_by_slot = jnp.transpose(a_rows, (0, 2, 1))
    rows_other = core_swap(rows_by_slot)

    along_z = exchange(copies, z_groups())
    beside = partner(along_z, "middle", 1)
    across = partner(along_z, "middle", 3)
    opposite = partner(across, "middle", 1)
    near, away = jnp.stack([along_z, beside]), jnp.stack([across, opposite])
    near_3 = partner(near, "last", 3)
    near, rows_other = lax.optimization_barrier((near, rows_other))
    slots, rows = plan(rows_by_slot, rows_other)
    near, away, slots, rows = lax.optimization_barrier((near, away, slots, rows))
    away_1 = partner(away, "last", 1)
    near_1 = partner(near, "last", 1)
    away_3 = partner(away, "last", 3)
    acc, both = sums(None, [(near, 0, NEAR), (away, 0, AWAY)], right, left)
    near_3, away_1, acc = lax.optimization_barrier((near_3, away_1, acc))
    near_2 = partner(near_3, "last", 1)
    away_2 = partner(away_1, "last", 3)
    (acc,) = sums(acc, [(near_3, 3, NEAR), (away_1, 1, AWAY)], right)
    acc, far = sums(
        acc, [(near_1, 1, NEAR), (away_3, 3, AWAY)], right, ahead=((2, NEAR), (2, AWAY))
    )
    keep, send = terms(slots, rows, left_sizes, right_sizes, acc, near_2, away_2, far, both)
    mine = (keep + core_swap(send).astype(jnp.float32)).astype(jnp.bfloat16)
    groups = [
        [flat(z, xh * NXL + xl, y, c) for z in range(NZ) for xh in range(NXH)]
        for c in range(NC)
        for xl in range(NXL)
        for y in range(NY)
    ]
    parts = exchange(mine, groups)
    return parts.astype(jnp.float32).sum(axis=0)


def solution(mesh):
    placed = (
        P("pair", "panel"),
        P("pair", None, None, None, None),
        P("pair", None, None),
        P("pair", "panel", None),
        P(),
        P(),
    )
    return jax.shard_map(
        local, mesh=mesh, in_specs=placed, out_specs=P("pair", "panel"), check_vma=False
    )
```
